256 devices in a mesh: dp: 32 (over y, z_lo, x), mp: 8 (over z_hi, core).
Axes of the slice: x: 4, y: 4, z: 8 (z_hi: 4, z_lo: 2; z = z_hi * 2 + z_lo), core: 2. Of those that a mesh axis runs over, the one named last changes fastest.
Arguments:
- enc_resid: bfloat16 [32, 256, 4096], P(None, 'dp', 'mp'), may hold values from -420 to 420
- enc_gain: float32 [4096], P('mp'), may hold values from 0.5 to 2
- text_in_w: bfloat16 [4096, 3072], P('mp'), may hold values from -0.09375 to 0.09375
- key_w: bfloat16 [3072, 3072], P('dp', 'mp'), may hold values from -0.109375 to 0.109375
- value_w: bfloat16 [3072, 3072], P('dp', 'mp'), may hold values from -0.109375 to 0.109375
- key_gain: float32 [128], replicated, may hold values from 0.5 to 2
- img_query: bfloat16 [24576, 3072], P('dp', 'mp'), may hold values from -24 to 24
- img_keys: bfloat16 [131072, 3072], P('dp', 'mp'), may hold values from -9 to 9
- img_values: bfloat16 [131072, 3072], P('dp', 'mp'), may hold values from -6 to 6
- out_grad: bfloat16 [24576, 3072], P('dp', 'mp'), may hold values from -6 to 6
- cap_lengths: int32 [32], replicated, may hold values from 32 to 256, as said below
- assignment: int32 [32], replicated, may hold values from 0 to 31, each once
Outputs:
- attn_out: float32 [24576, 3072], P('dp', 'mp')
- grad_key: float32 [3072, 3072], P('dp', 'mp')
- grad_value: float32 [3072, 3072], P('dp', 'mp')
The draws below stay inside these ranges and needn't reach their ends.
Inputs may be any that keep to these rules, and one draw needn't show every extreme that they name: `cap_lengths`: the longest caption fills all 256 positions in every draw.
All inputs are finite; a program needn't handle non-finite values.
Results may differ from the reference program's by a relative error of at most 0.017.
Values may be sent and summed in bfloat16 or wider, within the bound.
No kernel may reach another device: no remote copies, remote signals or barrier semaphores. Data moves between devices by JAX's collectives and lax.ppermute only.
A program may use at most 128 MiB of HBM per device.

```python
import math
import jax
import jax.numpy as jnp
from jax import lax

D_ENC = 4096
D = 3072
HD = 128
CT = 256
IQ = 768
IK = 4096
SAMPLES = 32


def shared_keys(key):
    normal_keys = jax.random.normal(jax.random.fold_in(key, 101), (SAMPLES * IK, D), jnp.float32)
    return jnp.clip(normal_keys, -3.0, 3.0)


def draw_img_keys(key, part):
    base = shared_keys(key)
    return base.astype(jnp.bfloat16)


def draw_img_query(key, part):
    key = jax.random.fold_in(key, 2)
    total_rows = SAMPLES * IQ
    entries = jnp.clip(jax.random.normal(key, (total_rows, D), jnp.float32), -3.0, 3.0)
    return (2.5 * entries).astype(jnp.bfloat16)


def draw_enc_resid(key, part):
    key = jax.random.fold_in(key, 3)
    first, second, third = jax.random.split(key, 3)
    row_scale = jnp.exp(jax.random.uniform(first, (SAMPLES, CT, 1), jnp.float32, 0.0, math.log(10.0)))
    ramp = 1.0 + 2.0 * jnp.arange(D_ENC, dtype=jnp.float32) / max(D_ENC - 1, 1)
    col_scale = jnp.exp(jax.random.uniform(second, (D_ENC,), jnp.float32, 0.0, math.log(10.0))) * ramp / 3.0
    base = jnp.clip(jax.random.normal(third, (SAMPLES, CT, D_ENC), jnp.float32), -4.0, 4.0)
    return (base * row_scale * col_scale).astype(jnp.bfloat16)


def draw_cap_lengths(key, part):
    key = jax.random.fold_in(key, 4)
    first, second = jax.random.split(key)
    drawn = jax.random.randint(first, (SAMPLES,), CT // 8, CT + 1, jnp.int32)
    picked = jax.random.randint(second, (), 0, SAMPLES, jnp.int32)
    return jnp.where(jnp.arange(SAMPLES, dtype=jnp.int32) == picked, CT, drawn).astype(jnp.int32)


def block_levels(rng, shape, cuts, smallest, largest):
    def one(position, shards_of):
        steps = jax.random.uniform(jax.random.fold_in(jax.random.fold_in(rng, 6), position), (shards_of,), jnp.float32, smallest / len(cuts), largest / len(cuts))
        return jnp.repeat(jnp.exp(steps), shape[position] // shards_of).reshape((-1,) + (1,) * (len(shape) - position - 1))

    loudness = one(*cuts[0])
    for cut in cuts[1:]:
        loudness = loudness * one(*cut)
    return loudness


def scatter_about(own_key, extent, width, reach, cuts=(), kind=jnp.bfloat16):
    loudness = block_levels(own_key, extent, cuts, -0.22, 0.18) if cuts else 1.0
    values = jax.random.normal(own_key, extent, jnp.float32) * width * loudness
    return jnp.minimum(jnp.maximum(values, -reach), reach).astype(kind)


def setup_inputs(seed: int = 0) -> dict:
    key_of = jax.random.split(jax.random.key(seed), 13)
    enc_resid = draw_enc_resid(jax.random.fold_in(key_of[12], 71), 0)
    enc_gain = jnp.clip(jnp.exp(math.log(2.0) - 1.3862944 * jax.random.uniform(key_of[1], (D_ENC,), jnp.float32) ** block_levels(key_of[1], (D_ENC,), ((0, 8),), -0.2, 0.2)), 0.5, 2.0)
    text_in_w = scatter_about(key_of[2], (D_ENC, D), D_ENC ** -0.5, 0.09375, ((0, 8),))
    key_w = scatter_about(key_of[3], (D, D), D ** -0.5, 0.109375, ((0, 32), (1, 8)))
    value_w = scatter_about(key_of[4], (D, D), D ** -0.5, 0.109375, ((0, 32), (1, 8)))
    key_gain = jnp.clip(jnp.exp(jax.random.uniform(key_of[5], (HD,), jnp.float32, math.log(0.5), math.log(2.0))), 0.5, 2.0)
    img_query = draw_img_query(jax.random.fold_in(key_of[12], 71), 0)
    img_keys = draw_img_keys(jax.random.fold_in(key_of[12], 71), 0)
    img_values = scatter_about(key_of[8], (SAMPLES * IK, D), 1.0, 6.0, ((0, 32), (1, 8)))
    out_grad = scatter_about(key_of[9], (SAMPLES * IQ, D), 1.0, 6.0, ((0, 32), (1, 8)))
    cap_lengths = draw_cap_lengths(jax.random.fold_in(key_of[12], 71), 0)
    assignment = jax.random.permutation(key_of[11], SAMPLES).astype(jnp.int32)
    return dict(enc_resid=enc_resid, enc_gain=enc_gain, text_in_w=text_in_w, key_w=key_w, value_w=value_w, key_gain=key_gain, img_query=img_query, img_keys=img_keys, img_values=img_values, out_grad=out_grad, cap_lengths=cap_lengths, assignment=assignment)


def final_norm(resid, gain):
    values = resid.astype(jnp.float32)
    mean_sq = lax.optimization_barrier(jnp.mean(values * values, axis=-1, keepdims=True))
    return (values * lax.rsqrt(mean_sq + 1e-06) * gain).astype(jnp.bfloat16)

def head_attend(key_pre, value_pre, queries, image_keys, image_values, keep, key_gain):
    scale = queries.shape[-1] ** (-0.5)
    mean_sq = lax.optimization_barrier(jnp.mean(key_pre * key_pre, axis=-1, keepdims=True))
    text_keys = (key_pre * lax.rsqrt(mean_sq + 1e-06) * key_gain).astype(jnp.bfloat16)
    text_values = value_pre.astype(jnp.bfloat16)
    text_scores = jnp.dot(queries, text_keys.T, preferred_element_type=jnp.float32) * scale
    text_scores = jnp.where(keep[None, :], text_scores, -1e+30)
    image_scores = jnp.dot(queries, image_keys.T, preferred_element_type=jnp.float32) * scale
    highest = jnp.maximum(lax.optimization_barrier(jnp.max(text_scores, axis=-1, keepdims=True)), lax.optimization_barrier(jnp.max(image_scores, axis=-1, keepdims=True)))
    highest = lax.stop_gradient(highest)
    text_exp = jnp.exp(text_scores - highest)
    image_exp = jnp.exp(image_scores - highest)
    totals = lax.optimization_barrier(jnp.sum(text_exp, axis=-1, keepdims=True)) + lax.optimization_barrier(jnp.sum(image_exp, axis=-1, keepdims=True))
    text_probs = (text_exp / totals).astype(jnp.bfloat16)
    image_probs = (image_exp / totals).astype(jnp.bfloat16)
    joined = jnp.dot(text_probs, text_values, preferred_element_type=jnp.float32)
    return joined + jnp.dot(image_probs, image_values, preferred_element_type=jnp.float32)

def split_heads(matrix, size):
    return matrix.reshape(matrix.shape[0], -1, size).transpose(1, 0, 2)

def join_heads(stack):
    return stack.transpose(1, 0, 2).reshape(stack.shape[1], -1)

def heads_backward(key_pre, value_pre, queries, image_keys, image_values, cotangent, keep, key_gain):
    size = key_gain.shape[0]

    def one_head(items):
        head_key, head_value, head_query, head_ikeys, head_ivalues, head_cot = items

        def attend(first, second):
            return head_attend(first, second, head_query, head_ikeys, head_ivalues, keep, key_gain)
        joined, pullback = jax.vjp(attend, head_key, head_value)
        key_cot, value_cot = pullback(head_cot.astype(jnp.float32))
        return (joined, key_cot.astype(jnp.bfloat16), value_cot.astype(jnp.bfloat16))
    stacked = (split_heads(key_pre, size), split_heads(value_pre, size), split_heads(queries, size), split_heads(image_keys, size), split_heads(image_values, size), split_heads(cotangent, size))
    outs, key_cots, value_cots = lax.map(one_head, stacked)
    return (join_heads(outs), join_heads(key_cots), join_heads(value_cots))

def reference(enc_resid, enc_gain, text_in_w, key_w, value_w, key_gain, img_query, img_keys, img_values, out_grad, cap_lengths, assignment):
    normed = final_norm(enc_resid, enc_gain)
    order = jnp.argsort(assignment).astype(jnp.int32)

    def per_sample(carry, sample):
        grad_k, grad_v = carry
        caption = lax.dynamic_index_in_dim(order, sample, 0, keepdims=False).astype(jnp.int32)
        tokens = lax.dynamic_index_in_dim(normed, caption, 0, keepdims=False)
        text_rows = jnp.dot(tokens, text_in_w, preferred_element_type=jnp.float32).astype(jnp.bfloat16)
        length = lax.dynamic_index_in_dim(cap_lengths, caption, 0, keepdims=False).astype(jnp.int32)
        keep = jnp.arange(CT, dtype=jnp.int32) < length
        key_pre = jnp.dot(text_rows, key_w, preferred_element_type=jnp.float32)
        value_pre = jnp.dot(text_rows, value_w, preferred_element_type=jnp.float32)
        qstart = (sample * IQ).astype(jnp.int32)
        kstart = (sample * IK).astype(jnp.int32)
        queries = lax.dynamic_slice_in_dim(img_query, qstart, IQ, 0)
        cotangent = lax.dynamic_slice_in_dim(out_grad, qstart, IQ, 0)
        image_keys = lax.dynamic_slice_in_dim(img_keys, kstart, IK, 0)
        image_values = lax.dynamic_slice_in_dim(img_values, kstart, IK, 0)
        joined, key_cot, value_cot = heads_backward(key_pre, value_pre, queries, image_keys, image_values, cotangent, keep, key_gain)
        term_k = jnp.dot(text_rows.T, key_cot, preferred_element_type=jnp.float32)
        term_v = jnp.dot(text_rows.T, value_cot, preferred_element_type=jnp.float32)
        return ((grad_k + term_k, grad_v + term_v), joined)
    start = (jnp.zeros((D, D), jnp.float32), jnp.zeros((D, D), jnp.float32))
    (grad_key, grad_value), joined = lax.scan(per_sample, start, jnp.arange(SAMPLES, dtype=jnp.int32))
    return (joined.reshape(SAMPLES * IQ, D), grad_key, grad_value)
```

```python
import functools
import math

import jax
import jax.numpy as jnp
from jax import lax
from jax.experimental import pallas as pl
from jax.experimental.pallas import tpu as pltpu
from jax.sharding import Mesh, PartitionSpec as P

BF16 = jnp.bfloat16
F32 = jnp.float32

D_ENC = 4096
D = 3072
HD = 128
CT = 256
IQ = 768
IK = 4096
SAMPLES = 32
NY, NZL, NX, NZH, NC = 4, 2, 4, 4, 2
TOK = CT // SAMPLES
FEAT = D_ENC // (NZH * NC)
COLS = D // (NZH * NC)
HEADS = COLS // HD
CHUNK = D // NY
HALF = CHUNK // NC
GROUP = NZL * NX
EXTRA = 128
WIDE = NY * HALF + EXTRA
SCALE = HD ** (-0.5)
LOG2E = math.log2(math.e)
NT = (((1,), (1,)), ((), ()))
TN = (((0,), (0,)), ((), ()))
VMEM_LIMIT = 56 * 2**20


def params():
    return pltpu.CompilerParams(vmem_limit_bytes=VMEM_LIMIT)


def dot(a, b, dims=(((1,), (0,)), ((), ()))):
    return lax.dot_general(a, b, dims, preferred_element_type=F32)


def hi_lo(total, width):
    hi = total.astype(BF16)
    lo = (total - hi.astype(F32)).astype(BF16)
    lane = lax.broadcasted_iota(jnp.int32, (total.shape[0], width), 1)
    wide_hi = jnp.broadcast_to(hi.astype(F32), lane.shape)
    wide_lo = jnp.broadcast_to(lo.astype(F32), lane.shape)
    return jnp.where(lane == 0, wide_hi, jnp.where(lane == 1, wide_lo, 0.0)).astype(BF16)


def front_kernel(core_ref, assign_ref, x_ref, gain_ref, w_ref, send_ref, keep_ref, rows):
    step = pl.program_id(0)

    @pl.when(step == 0)
    def _():
        gain = gain_ref[...]
        for c in range(SAMPLES):
            start = pl.multiple_of(assign_ref[c] * TOK, TOK)
            values = x_ref[c].astype(F32)
            squares = jnp.sum(values * values, axis=1, keepdims=True)
            rows[pl.ds(start, TOK), :FEAT] = values * gain
            rows[pl.ds(start, TOK), FEAT:] = jnp.broadcast_to(squares, (TOK, EXTRA))
        total = rows[:, FEAT : FEAT + 1]
        send_ref[:, NY * HALF :] = hi_lo(total, EXTRA)
        lane = lax.broadcasted_iota(jnp.int32, (CT, EXTRA), 1)
        keep_ref[:, NY * HALF :] = jnp.where(lane == 0, rows[:, FEAT:], 0.0)

    part = dot(rows[:, :FEAT].astype(BF16), w_ref[...])
    for j in range(NY):

        @pl.when(step == j)
        def _():
            send_ref[:, j * HALF : (j + 1) * HALF] = part.astype(BF16)

        @pl.when(step == NY + j)
        def _():
            keep_ref[:, j * HALF : (j + 1) * HALF] = part


def front(core, assignment, x, gain, w):
    def column(i, core_ref, assign_ref):
        half = jnp.where(i < NY, 1 - core_ref[0], core_ref[0])
        return (0, (i % NY) * NC + half)

    whole = lambda *zeros: lambda i, *_: zeros
    return pl.pallas_call(
        front_kernel,
        grid_spec=pltpu.PrefetchScalarGridSpec(
            num_scalar_prefetch=2,
            grid=(NY * NC,),
            in_specs=[
                pl.BlockSpec((SAMPLES, TOK, FEAT), whole(0, 0, 0)),
                pl.BlockSpec((1, FEAT), whole(0, 0)),
                pl.BlockSpec((FEAT, HALF), column),
            ],
            out_specs=[
                pl.BlockSpec((CT, WIDE), whole(0, 0)),
                pl.BlockSpec((CT, WIDE), whole(0, 0)),
            ],
            scratch_shapes=[pltpu.VMEM((CT, FEAT + EXTRA), F32)],
        ),
        out_shape=[
            jax.ShapeDtypeStruct((CT, WIDE), BF16),
            jax.ShapeDtypeStruct((CT, WIDE), F32),
        ],
        compiler_params=params(),
        name="text_partial",
    )(core, assignment, x, gain, w)


def core_sum_kernel(keep_ref, got_ref, out_ref):
    total = keep_ref[...] + got_ref[...].astype(F32)
    edge = NY * HALF
    squares = jnp.sum(total[:, edge:], axis=1, keepdims=True)
    out_ref[:, :edge] = total[:, :edge].astype(BF16)
    out_ref[:, edge:] = hi_lo(squares, EXTRA)


def core_sum(keep, got):
    return pl.pallas_call(
        core_sum_kernel,
        out_shape=jax.ShapeDtypeStruct((CT, WIDE), BF16),
        compiler_params=params(),
        name="core_sum",
    )(keep, got)


def text_kernel(got_ref, out_ref):
    total = got_ref[0].astype(F32)
    for i in range(1, NZH):
        total = total + got_ref[i].astype(F32)
    edge = NY * HALF
    squares = jnp.sum(total[:, edge:], axis=1, keepdims=True)
    scale = lax.rsqrt(squares / D_ENC + 1e-06)
    for j in range(NY):
        out_ref[j] = (total[:, j * HALF : (j + 1) * HALF] * scale).astype(BF16)


def finish_text(got):
    rows = CT // NZH
    return pl.pallas_call(
        text_kernel,
        out_shape=jax.ShapeDtypeStruct((NY, rows, HALF), BF16),
        compiler_params=params(),
        name="finish_text",
    )(got)


def project_kernel(core_ref, own_ref, other_ref, w_ref, out_ref):
    core = core_ref[0]
    own_w = w_ref[pl.ds(pl.multiple_of(core * HALF, HALF), HALF), :]
    other_w = w_ref[pl.ds(pl.multiple_of((1 - core) * HALF, HALF), HALF), :]
    out_ref[...] = (dot(own_ref[...], own_w) + dot(other_ref[...], other_w)).astype(BF16)


def project(core, own, other, w):
    return pl.pallas_call(
        project_kernel,
        grid_spec=pltpu.PrefetchScalarGridSpec(
            num_scalar_prefetch=1,
            grid=(NY,),
            in_specs=[
                pl.BlockSpec((CT, HALF), lambda i, _: (i, 0)),
                pl.BlockSpec((CT, HALF), lambda i, _: (i, 0)),
                pl.BlockSpec((CHUNK, 2 * COLS), lambda i, _: (0, 0)),
            ],
            out_specs=pl.BlockSpec((CT, 2 * COLS), lambda i, _: (i, 0)),
        ),
        out_shape=jax.ShapeDtypeStruct((NY * CT, 2 * COLS), BF16),
        compiler_params=params(),
        name="project",
    )(core, own, other, w)


def image_kernel(q_ref, k_ref, v_ref, o_ref, m_ref, l_ref, wide, *, block, rows):
    factor = SCALE * LOG2E
    wide[:, :HD] = v_ref[...]
    wide[:, HD:] = jnp.ones((IK, HD), BF16)
    for r in range(IQ // rows):
        part = pl.ds(r * rows, rows)
        q = q_ref[part, :]
        top = None
        for j in range(IK // block):
            cols = pl.ds(j * block, block)
            s = dot(q, k_ref[cols, :], NT)
            here = jnp.max(s, axis=1, keepdims=True) * factor
            new = here if top is None else jnp.maximum(top, here)
            p = jnp.exp2(s * factor - new).astype(BF16)
            add = dot(p, wide[cols, :])
            acc = add if top is None else acc * jnp.exp2(top - new) + add
            top = new
        o_ref[part, :] = acc[:, :HD]
        l_ref[part, :] = acc[:, HD:]
        m_ref[part, :] = jnp.broadcast_to(top, (rows, HD))


def image_attention(q, k, v, head):
    out = jax.ShapeDtypeStruct((IQ, HD), F32)
    return pl.pallas_call(
        functools.partial(image_kernel, block=512, rows=256),
        grid=(1,),
        in_specs=[
            pl.BlockSpec((IQ, HD), lambda i: (0, head)),
            pl.BlockSpec((IK, HD), lambda i: (0, head)),
            pl.BlockSpec((IK, HD), lambda i: (0, head)),
        ],
        out_specs=[pl.BlockSpec((IQ, HD), lambda i: (0, 0))] * 3,
        out_shape=[out] * 3,
        scratch_shapes=[pltpu.VMEM((IK, 2 * HD), BF16)],
        compiler_params=params(),
        name="image_attention",
    )(q, k, v)


def text_attention_kernel(
    length_ref, kv_ref, q_ref, g_ref, gain_ref, *refs
):
    parts, (out_ref, cot_ref) = refs[: 3 * HEADS], refs[3 * HEADS :]
    length = length_ref[0]
    gain = gain_ref[...]
    factor = SCALE * LOG2E
    keep = lax.broadcasted_iota(jnp.int32, (1, CT), 1) < length
    kv = kv_ref[0].astype(F32)
    for i in range(1, NY):
        kv = kv + kv_ref[i].astype(F32)
    for h in range(HEADS):
        cols = slice(h * HD, (h + 1) * HD)
        o, m, l = parts[3 * h][...], parts[3 * h + 1][:, :1], parts[3 * h + 2][:, :1]
        key_pre = kv[:, cols]
        value = kv[:, COLS + h * HD : COLS + (h + 1) * HD].astype(BF16)
        root = lax.rsqrt(jnp.mean(key_pre * key_pre, axis=1, keepdims=True) + 1e-06)
        key = (key_pre * root * gain).astype(BF16)
        q = q_ref[:, cols]
        g = g_ref[:, cols]
        s = jnp.where(keep, dot(q, key, NT) * factor, -1e30)
        top = jnp.maximum(m, jnp.max(s, axis=1, keepdims=True))
        e = jnp.exp2(s - top)
        fade = jnp.exp2(m - top)
        inverse = 1.0 / (l * fade + jnp.sum(e, axis=1, keepdims=True))
        p = e * inverse
        probs = p.astype(BF16)
        joint = o * (fade * inverse) + dot(probs, value)
        out_ref[:, cols] = joint
        mean = jnp.sum(g.astype(F32) * joint, axis=1, keepdims=True)
        dp = dot(g, value, NT)
        ds = (p * (dp - mean) * SCALE).astype(BF16)
        d_value = dot(probs, g, TN).astype(BF16)
        d_key = dot(ds, q, TN).astype(BF16).astype(F32) * gain
        along = jnp.mean(d_key * key_pre, axis=1, keepdims=True)
        d_pre = (root * d_key - key_pre * (root * root * root * along)).astype(BF16)
        for i in range(NY):
            cot_ref[i, :, cols] = d_pre
            cot_ref[i, :, COLS + h * HD : COLS + (h + 1) * HD] = d_value


def text_attention(length, kv, q, g, gain, parts):
    vmem = pl.BlockSpec(memory_space=pltpu.VMEM)
    return pl.pallas_call(
        text_attention_kernel,
        in_specs=[pl.BlockSpec(memory_space=pltpu.SMEM)] + [vmem] * (4 + 3 * HEADS),
        out_specs=[vmem, vmem],
        out_shape=[
            jax.ShapeDtypeStruct((IQ, COLS), F32),
            jax.ShapeDtypeStruct((NY, CT, 2 * COLS), BF16),
        ],
        compiler_params=params(),
        name="text_attention",
    )(length, kv, q, g, gain, *parts)


def gradient_kernel(core_ref, own_ref, other_ref, cot_ref, out_ref):
    step = pl.program_id(0)

    @pl.when(step == 0)
    def _():
        out_ref[...] = dot(own_ref[...], cot_ref[...], TN).astype(BF16)

    @pl.when(step == 1)
    def _():
        out_ref[...] = dot(other_ref[...], cot_ref[...], TN).astype(BF16)


def gradient(core, own, other, cot):
    whole = lambda i, _: (0, 0)
    return pl.pallas_call(
        gradient_kernel,
        grid_spec=pltpu.PrefetchScalarGridSpec(
            num_scalar_prefetch=1,
            grid=(NC,),
            in_specs=[
                pl.BlockSpec((NY * CT, HALF), whole),
                pl.BlockSpec((NY * CT, HALF), whole),
                pl.BlockSpec((NY * CT, 2 * COLS), whole),
            ],
            out_specs=pl.BlockSpec(
                (HALF, 2 * COLS), lambda i, c: (jnp.where(i == 0, c[0], 1 - c[0]), 0)
            ),
        ),
        out_shape=jax.ShapeDtypeStruct((CHUNK, 2 * COLS), BF16),
        compiler_params=params(),
        name="gradient",
    )(core, own, other, cot)


def body(
    enc_resid,
    enc_gain,
    text_in_w,
    key_w,
    value_w,
    key_gain,
    img_query,
    img_keys,
    img_values,
    out_grad,
    cap_lengths,
    assignment,
):
    core = lax.axis_index("c").astype(jnp.int32).reshape(1)
    sample = (lax.axis_index("y") * NZL + lax.axis_index("zl")) * NX + lax.axis_index("x")
    length = jnp.sum(jnp.where(assignment == sample, cap_lengths, 0)).reshape(1)
    swap = [(0, 1), (1, 0)]

    both_w = lax.all_gather(
        jnp.concatenate([key_w, value_w], axis=1), ("zl", "x"), axis=0, tiled=True
    )

    send, keep = front(core, assignment, enc_resid, enc_gain.reshape(1, FEAT), text_in_w)
    summed = core_sum(keep, lax.ppermute(send, "c", swap))

    parts = []

    def beside(operand, move, head):
        operand, query = lax.optimization_barrier((operand, img_query))
        moved = move(operand)
        part = image_attention(query, img_keys, img_values, head)
        moved, part = lax.optimization_barrier((moved, tuple(part)))
        parts.extend(part)
        return moved

    got = beside(
        summed.reshape(NZH, CT // NZH, WIDE),
        lambda a: lax.all_to_all(a, "zh", 0, 0, tiled=True),
        0,
    )
    text = finish_text(got).reshape(SAMPLES, TOK, HALF)
    text = lax.all_to_all(text, ("y", "zl", "x"), 0, 0, tiled=True)
    spread = jnp.broadcast_to(text.reshape(1, CT, HALF), (NZH, CT, HALF))
    own = beside(spread, lambda a: lax.all_to_all(a, "zh", 0, 0, tiled=True), 1)
    own = own.reshape(NY * CT, HALF)
    other = lax.ppermute(own, "c", swap)
    kv = project(core, own, other, both_w)
    kv = beside(
        kv.reshape(NY, CT, 2 * COLS), lambda a: lax.all_to_all(a, "y", 0, 0, tiled=True), 2
    )
    attn_out, cot = text_attention(
        length, kv, img_query, out_grad, key_gain.reshape(1, HD), parts
    )
    cot = lax.all_to_all(cot, "y", 0, 0, tiled=True).reshape(NY * CT, 2 * COLS)
    grad = gradient(core, own, other, cot).reshape(GROUP, D // SAMPLES, 2 * COLS)
    grad = lax.all_to_all(grad, ("zl", "x"), 0, 0, tiled=True)
    total = jnp.sum(grad.astype(F32), axis=0)
    return (attn_out, total[:, :COLS], total[:, COLS:])


def solution(mesh):
    fine = Mesh(mesh.devices.reshape(NY, NZL, NX, NZH, NC), ("y", "zl", "x", "zh", "c"))
    dp, mp = ("y", "zl", "x"), ("zh", "c")
    return jax.shard_map(
        body,
        mesh=fine,
        in_specs=(
            P(None, dp, mp),
            P(mp),
            P(mp, None),
            P(dp, mp),
            P(dp, mp),
            P(),
            P(dp, mp),
            P(dp, mp),
            P(dp, mp),
            P(dp, mp),
            P(),
            P(),
        ),
        out_specs=(P(dp, mp), P(dp, mp), P(dp, mp)),
        check_vma=False,
    )
```

```python
import functools
import math

import jax
import jax.numpy as jnp
from jax import lax
from jax.experimental import pallas as pl
from jax.experimental.pallas import tpu as pltpu
from jax.sharding import Mesh, PartitionSpec as P

BF16 = jnp.bfloat16
F32 = jnp.float32

D_ENC = 4096
D = 3072
HD = 128
CT = 256
IQ = 768
IK = 4096
SAMPLES = 32
NY, NZL, NX, NZH, NC = 4, 2, 4, 4, 2
TOK = CT // SAMPLES
FEAT = D_ENC // (NZH * NC)
COLS = D // (NZH * NC)
HEADS = COLS // HD
CHUNK = D // NY
HALF = CHUNK // NC
GROUP = NZL * NX
IMAGE_MIB = 56
WROWS = D // SAMPLES
EXTRA = 16
ROWS = CT + EXTRA
SCALE = HD ** (-0.5)
LOG2E = math.log2(math.e)
NT = (((1,), (1,)), ((), ()))
TN = (((0,), (0,)), ((), ()))


def params(mib):
    return pltpu.CompilerParams(vmem_limit_bytes=mib * 2**20)


def dot(a, b, dims=(((1,), (0,)), ((), ()))):
    return lax.dot_general(a, b, dims, preferred_element_type=F32)


def square_rows(total):
    hi = total.astype(BF16).astype(F32)
    full = jnp.concatenate([total, jnp.zeros((1, HALF - CT), F32)], axis=1)
    top = jnp.concatenate([hi, jnp.zeros((1, HALF - CT), F32)], axis=1)
    row = lax.broadcasted_iota(jnp.int32, (EXTRA, HALF), 0)
    return jnp.where(row == 0, top, jnp.where(row == 1, full - top, 0.0)).astype(BF16)


def read_squares(block):
    return jnp.sum(block[:, :CT].astype(F32), axis=0, keepdims=True)


def prepare_kernel(assign_ref, x_ref, gain_ref, xg_ref, sq_ref, rows, squares):
    gain = gain_ref[...]
    for c in range(SAMPLES):
        start = pl.multiple_of(assign_ref[c] * TOK, TOK)
        values = x_ref[c].astype(F32)
        rows[pl.ds(start, TOK), :] = values * gain
        squares[pl.ds(start, TOK), :] = jnp.broadcast_to(
            jnp.sum(values * values, axis=1, keepdims=True), (TOK, 128)
        )
    xg_ref[...] = rows[...].astype(BF16)
    sq_ref[...] = squares[...].T[:8, :]


def prepare(assignment, x, gain):
    vmem = pl.BlockSpec(memory_space=pltpu.VMEM)
    return pl.pallas_call(
        prepare_kernel,
        in_specs=[pl.BlockSpec(memory_space=pltpu.SMEM), vmem, vmem],
        out_specs=[vmem, vmem],
        out_shape=[jax.ShapeDtypeStruct((CT, FEAT), BF16), jax.ShapeDtypeStruct((8, CT), F32)],
        scratch_shapes=[pltpu.VMEM((CT, FEAT), F32), pltpu.VMEM((CT, 128), F32)],
        compiler_params=params(8),
        name="prepare",
    )(assignment, x, gain)


def send_kernel(core_ref, xg_ref, sq_ref, w_ref, out_ref):
    out_ref[0, :CT, :] = dot(xg_ref[...], w_ref[...]).astype(BF16)
    out_ref[0, CT:, :] = square_rows(sq_ref[:1, :])


def send_part(core, xg, sq, w):
    return pl.pallas_call(
        send_kernel,
        grid_spec=pltpu.PrefetchScalarGridSpec(
            num_scalar_prefetch=1,
            grid=(NZH,),
            in_specs=[
                pl.BlockSpec((CT, FEAT), lambda i, _: (0, 0)),
                pl.BlockSpec((8, CT), lambda i, _: (0, 0)),
                pl.BlockSpec((FEAT, HALF), lambda i, c: (0, i * NC + 1 - c[0])),
            ],
            out_specs=pl.BlockSpec((1, ROWS, HALF), lambda i, _: (i, 0, 0)),
        ),
        out_shape=jax.ShapeDtypeStruct((NZH, ROWS, HALF), BF16),
        compiler_params=params(16),
        name="text_other_half",
    )(core, xg, sq, w)


def keep_kernel(core_ref, xg_ref, sq_ref, w_ref, got_ref, out_ref):
    total = dot(xg_ref[...], w_ref[...]) + got_ref[0, :CT, :].astype(F32)
    out_ref[0, :CT, :] = total.astype(BF16)
    out_ref[0, CT:, :] = square_rows(sq_ref[:1, :] + read_squares(got_ref[0, CT:, :]))


def keep_part(core, xg, sq, w, got):
    block = pl.BlockSpec((1, ROWS, HALF), lambda i, _: (i, 0, 0))
    return pl.pallas_call(
        keep_kernel,
        grid_spec=pltpu.PrefetchScalarGridSpec(
            num_scalar_prefetch=1,
            grid=(NZH,),
            in_specs=[
                pl.BlockSpec((CT, FEAT), lambda i, _: (0, 0)),
                pl.BlockSpec((8, CT), lambda i, _: (0, 0)),
                pl.BlockSpec((FEAT, HALF), lambda i, c: (0, i * NC + c[0])),
                block,
            ],
            out_specs=block,
        ),
        out_shape=jax.ShapeDtypeStruct((NZH, ROWS, HALF), BF16),
        compiler_params=params(16),
        name="text_own_half",
    )(core, xg, sq, w, got)


def text_kernel(got_ref, out_ref):
    total = got_ref[0].astype(F32)
    for i in range(1, NZH):
        total = total + got_ref[i].astype(F32)
    scale = lax.rsqrt(read_squares(total[CT:, :]) / D_ENC + 1e-06)
    column = jnp.broadcast_to(scale, (128, CT)).T[:, :1]
    out_ref[...] = (total[:CT, :] * column).astype(BF16)


def finish_text(got):
    return pl.pallas_call(
        text_kernel,
        out_shape=jax.ShapeDtypeStruct((CT, HALF), BF16),
        compiler_params=params(16),
        name="finish_text",
    )(got)


def image_kernel(q_ref, k_ref, v_ref, *refs, block, rows):
    o_ref, ml_ref, wide = refs[-3:]
    factor = SCALE * LOG2E
    wide[:, :HD] = v_ref[...]
    wide[:, HD:] = jnp.ones((IK, HD), BF16)
    lane = lax.broadcasted_iota(jnp.int32, (rows, HD), 1)
    for r in range(IQ // rows):
        part = pl.ds(r * rows, rows)
        q = q_ref[part, :]
        top = None
        for j in range(IK // block):
            cols = pl.ds(j * block, block)
            s = dot(q, k_ref[cols, :], NT)
            here = jnp.max(s, axis=1, keepdims=True) * factor
            new = here if top is None else jnp.maximum(top, here)
            p = jnp.exp2(s * factor - new).astype(BF16)
            add = dot(p, wide[cols, :])
            acc = add if top is None else acc * jnp.exp2(top - new) + add
            top = new
        o_ref[part, :] = acc[:, :HD]
        ml_ref[part, :] = jnp.where(lane < HD // 2, top, acc[:, HD:])


def image_attention(q, k, v, heads, before):
    column = lambda i: (0, heads[0] + i)
    return pl.pallas_call(
        functools.partial(image_kernel, block=512, rows=256),
        grid=(len(heads),),
        in_specs=[
            pl.BlockSpec((IQ, HD), column),
            pl.BlockSpec((IK, HD), column),
            pl.BlockSpec((IK, HD), column),
        ]
        + [pl.BlockSpec(memory_space=pl.ANY)] * len(before),
        out_specs=[pl.BlockSpec((IQ, HD), column)] * 2,
        out_shape=[jax.ShapeDtypeStruct((IQ, COLS), F32)] * 2,
        scratch_shapes=[pltpu.VMEM((IK, 2 * HD), BF16)],
        input_output_aliases={3 + i: i for i in range(len(before))},
        cost_estimate=pl.CostEstimate(flops=1, bytes_accessed=1, transcendentals=0),
        compiler_params=params(IMAGE_MIB),
        name="image_attention",
    )(q, k, v, *before)


def head_attention(length, key_pre, value_pre, q, g, gain, image_sum, stats):
    factor = SCALE * LOG2E
    keep = lax.broadcasted_iota(jnp.int32, (CT, 1), 0) < length
    turned = stats.T
    m, l = turned[:1, :], turned[HD // 2 : HD // 2 + 1, :]
    value = value_pre.astype(BF16)
    root = lax.rsqrt(jnp.mean(key_pre * key_pre, axis=1, keepdims=True) + 1e-06)
    key = (key_pre * root * gain).astype(BF16)
    s = jnp.where(keep, dot(key, q, NT) * factor, -1e30)
    top = jnp.maximum(m, jnp.max(s, axis=0, keepdims=True))
    e = jnp.exp2(s - top)
    fade = jnp.exp2(m - top)
    inverse = 1.0 / (l * fade + jnp.sum(e, axis=0, keepdims=True))
    p = e * inverse
    probs = p.astype(BF16)
    image_scale = jnp.broadcast_to(fade * inverse, (HD, IQ)).T
    joint = image_sum * image_scale + dot(probs, value, TN)
    mean = jnp.sum((g.astype(F32) * joint).T, axis=0, keepdims=True)
    ds = (p * (dot(value, g, NT) - mean) * SCALE).astype(BF16)
    d_value = dot(probs, g).astype(BF16)
    d_key = dot(ds, q).astype(BF16).astype(F32) * gain
    along = jnp.mean(d_key * key_pre, axis=1, keepdims=True)
    d_pre = (root * d_key - key_pre * (root * root * root * along)).astype(BF16)
    return joint, d_pre, d_value


def text_side_kernel(length_ref, place_ref, gain_ref, *refs):
    whole, blocks = refs[:6], refs[6 : 6 + NY + NX]
    out_ref, cot_ref = refs[6 + NY + NX : 8 + NY + NX]
    local = refs[8 + NY + NX : 14 + NY + NX]
    w, kv, joined, cots, in_sems, w_sems, out_sems, cot_sems = refs[14 + NY + NX :]
    own, other, q, g, image_sum, stats = local
    y, zl, x, core = (place_ref[i] for i in range(4))

    fetch = [
        pltpu.make_async_copy(source, target, in_sems.at[i])
        for i, (source, target) in enumerate(zip(whole, local))
    ]
    for i in range(2):
        fetch[i].start()
    order = (0, 1, 3, 2)
    moves = {s: [] for s in order}
    for s in order:
        for n in range(2):
            for r in range(NX):
                far, near = (s, r) if n == 0 else (r, s)
                for t in range(NZL):
                    half = zl if t == 0 else 1 - zl
                    target = w.at[s, half, (x + NX - r) % NX, :, n * COLS : (n + 1) * COLS]
                    source = blocks[n * 4 + far].at[near, t]
                    move = pltpu.make_async_copy(source, target, w_sems.at[s, len(moves[s])])
                    move.start()
                    moves[s].append(move)
    for i in range(2, 6):
        fetch[i].start()

    for i in range(2):
        fetch[i].wait()
    for s in order:
        for move in moves[s]:
            move.wait()
        plane = (y + NY - s) % NY
        own_w = w[s, core].reshape(HALF, 2 * COLS)
        other_w = w[s, 1 - core].reshape(HALF, 2 * COLS)
        part = dot(own[plane], own_w) + dot(other[plane], other_w)
        if s == 0:
            kv[...] = part
        else:
            kv[...] += part

    for i in range(2, 6):
        fetch[i].wait()
    leave = []
    for h in range(HEADS):
        cols = slice(h * HD, (h + 1) * HD)
        joint, d_pre, d_value = head_attention(
            length_ref[0],
            kv[:, cols],
            kv[:, COLS + h * HD : COLS + (h + 1) * HD],
            q[:, cols],
            g[:, cols],
            gain_ref[...],
            image_sum[:, cols],
            stats[:, cols],
        )
        for n, value in ((0, d_pre), (1, d_value)):
            span = slice(n * COLS + h * HD, n * COLS + (h + 1) * HD)
            cots[:, span] = value
            for i in range(NY):
                leave.append(
                    pltpu.make_async_copy(
                        cots.at[:, span], cot_ref.at[i, :, span], cot_sems.at[h, n, i]
                    )
                )
                leave[-1].start()
        joined[:, cols] = joint
        leave.append(
            pltpu.make_async_copy(joined.at[:, cols], out_ref.at[:, cols], out_sems.at[h])
        )
        leave[-1].start()
    for move in leave:
        move.wait()


def text_side(length, place, gain, own, other, q, g, image_sum, stats, keys, values):
    smem = pl.BlockSpec(memory_space=pltpu.SMEM)
    anywhere = pl.BlockSpec(memory_space=pl.ANY)
    whole = [own, other, q, g, image_sum, stats]
    return pl.pallas_call(
        text_side_kernel,
        in_specs=[smem, smem, pl.BlockSpec(memory_space=pltpu.VMEM)]
        + [anywhere] * (len(whole) + NY + NX),
        out_specs=[anywhere, anywhere],
        out_shape=[
            jax.ShapeDtypeStruct((IQ, COLS), F32),
            jax.ShapeDtypeStruct((NY, CT, 2 * COLS), BF16),
        ],
        scratch_shapes=[pltpu.VMEM(a.shape, a.dtype) for a in whole]
        + [
            pltpu.VMEM((NY, NZL, NX, WROWS, 2 * COLS), BF16),
            pltpu.VMEM((CT, 2 * COLS), F32),
            pltpu.VMEM((IQ, COLS), F32),
            pltpu.VMEM((CT, 2 * COLS), BF16),
            pltpu.SemaphoreType.DMA((len(whole),)),
            pltpu.SemaphoreType.DMA((NY, 2 * NX * NZL)),
            pltpu.SemaphoreType.DMA((HEADS,)),
            pltpu.SemaphoreType.DMA((HEADS, 2, NY)),
        ],
        compiler_params=params(56),
        name="text_side",
    )(length, place, gain, *whole, *keys, *values)


def turn_kernel(core_ref, own_ref, other_ref, out_ref):
    core = core_ref[0]
    for i, ref in ((0, own_ref), (1, other_ref)):
        half = core if i == 0 else 1 - core
        out_ref[pl.ds(pl.multiple_of(half * HALF, HALF), HALF), :] = ref[...].T


def turn(core, own, other):
    return pl.pallas_call(
        turn_kernel,
        in_specs=[pl.BlockSpec(memory_space=pltpu.SMEM)]
        + [pl.BlockSpec(memory_space=pltpu.VMEM)] * 2,
        out_shape=jax.ShapeDtypeStruct((CHUNK, NY * CT), BF16),
        compiler_params=params(16),
        name="turn_text",
    )(core, own, other)


def gradient_kernel(text_ref, cot_ref, out_ref):
    out_ref[...] = dot(text_ref[...], cot_ref[...]).astype(BF16)


def gradient(text, cot):
    steps = 2
    return pl.pallas_call(
        gradient_kernel,
        grid=(steps,),
        in_specs=[
            pl.BlockSpec((CHUNK // steps, NY * CT), lambda i: (i, 0)),
            pl.BlockSpec((NY * CT, 2 * COLS), lambda i: (0, 0)),
        ],
        out_specs=pl.BlockSpec((CHUNK // steps, 2 * COLS), lambda i: (i, 0)),
        out_shape=jax.ShapeDtypeStruct((CHUNK, 2 * COLS), BF16),
        compiler_params=params(16),
        name="gradient",
    )(text, cot)


def body(
    enc_resid,
    enc_gain,
    text_in_w,
    key_w,
    value_w,
    key_gain,
    img_query,
    img_keys,
    img_values,
    out_grad,
    cap_lengths,
    assignment,
):
    core = lax.axis_index("c").astype(jnp.int32).reshape(1)
    zl = lax.axis_index("zl")
    sample = (lax.axis_index("y") * NZL + zl) * NX + lax.axis_index("x")
    length = jnp.sum(jnp.where(assignment == sample, cap_lengths, 0)).reshape(1)
    swap = [(0, 1), (1, 0)]
    tie = lax.optimization_barrier

    place = jnp.stack([lax.axis_index(n).astype(jnp.int32) for n in ("y", "zl", "x", "c")])

    def ring(step):
        return [(i, (i + step) % 4) for i in range(4)]

    def image(heads, query, before=()):
        return tuple(image_attention(query, img_keys, img_values, heads, before))

    def around(pair, axis):
        block = jnp.stack(pair)
        two, one, three = [lax.ppermute(block, axis, ring(k)) for k in (2, 1, 3)]
        return [block, one, two, three]

    def beside(block, axis):
        return [lax.ppermute(block, axis, ring(k)) for k in (1, 3)]

    key_pair = [key_w, lax.ppermute(key_w, "zl", swap)]
    value_pair = [value_w, lax.ppermute(value_w, "zl", swap)]

    xg, sq = prepare(assignment, enc_resid, enc_gain.reshape(1, FEAT))
    send = send_part(core, xg, sq, text_in_w)
    summed = keep_part(core, xg, sq, text_in_w, lax.ppermute(send, "c", swap))

    summed, key_pair, value_pair, query = tie((summed, key_pair, value_pair, img_query))
    got = lax.all_to_all(summed, "zh", 0, 0, tiled=True)
    key_x = around(key_pair, "x")
    value_y = around(value_pair, "y")
    part = image((0,), query)
    got, key_x, value_y, length, place, part = tie((got, key_x, value_y, length, place, part))

    text = finish_text(got).reshape(SAMPLES, TOK, HALF)
    text, key_x, value_y, part, query = tie(
        (text, jnp.stack(key_x), jnp.stack(value_y), part, img_query)
    )
    text = lax.all_to_all(text, ("y", "zl", "x"), 0, 0, tiled=True)
    key_1, key_3 = beside(key_x, "y")
    value_1, value_3 = beside(value_y, "x")
    text, key_1, key_3, value_1, value_3 = tie((text, key_1, key_3, value_1, value_3))
    spread = jnp.broadcast_to(text.reshape(1, CT, HALF), (NZH, CT, HALF))
    spread, query, part = tie((spread, query, part))
    own = lax.all_to_all(spread, "zh", 0, 0, tiled=True)
    key_2 = lax.ppermute(key_1, "y", ring(1))
    value_2 = lax.ppermute(value_3, "x", ring(3))
    part = image((1, 2), query, part)
    own, (o, ml), key_2, value_2 = tie((own, part, key_2, value_2))
    other = lax.ppermute(own, "c", swap)
    own_group = lax.all_to_all(own, "y", 0, 0, tiled=True).reshape(NY * CT, HALF)
    attn_out, cot = text_side(
        length,
        place,
        key_gain.reshape(1, HD),
        own,
        other,
        img_query,
        out_grad,
        o,
        ml,
        (key_x, key_1, key_2, key_3),
        (value_y, value_1, value_2, value_3),
    )
    cot, own_group = tie((cot, own_group))
    other_group = lax.ppermute(own_group, "c", swap)
    cot = lax.all_to_all(cot, "y", 0, 0, tiled=True)
    turned = turn(core, own_group, other_group)
    cot, turned = tie((cot, turned))
    cot = cot.reshape(NY * CT, 2 * COLS)
    grad = gradient(turned, cot).reshape(GROUP, WROWS, 2 * COLS)
    grad = lax.all_to_all(grad, ("zl", "x"), 0, 0, tiled=True)
    total = jnp.sum(grad.astype(F32), axis=0)
    return (attn_out, total[:, :COLS], total[:, COLS:])


def solution(mesh):
    fine = Mesh(mesh.devices.reshape(NY, NZL, NX, NZH, NC), ("y", "zl", "x", "zh", "c"))
    dp, mp = ("y", "zl", "x"), ("zh", "c")
    return jax.shard_map(
        body,
        mesh=fine,
        in_specs=(
            P(None, dp, mp),
            P(mp),
            P(mp, None),
            P(dp, mp),
            P(dp, mp),
            P(),
            P(dp, mp),
            P(dp, mp),
            P(dp, mp),
            P(dp, mp),
            P(),
            P(),
        ),
        out_specs=(P(dp, mp), P(dp, mp), P(dp, mp)),
        check_vma=False,
    )
```

```python
import functools
import math

import jax
import jax.numpy as jnp
from jax import lax
from jax.experimental import pallas as pl
from jax.experimental.pallas import tpu as pltpu
from jax.sharding import Mesh, PartitionSpec as P

BF16 = jnp.bfloat16
F32 = jnp.float32

D_ENC = 4096
D = 3072
HD = 128
CT = 256
IQ = 768
IK = 4096
SAMPLES = 32
NY, NZL, NX, NZH, NC = 4, 2, 4, 4, 2
TOK = CT // SAMPLES
FEAT = D_ENC // (NZH * NC)
COLS = D // (NZH * NC)
HEADS = COLS // HD
CHUNK = D // NY
HALF = CHUNK // NC
GROUP = NZL * NX
IMAGE_MIB = 56
SORT_MIB = 56
FETCH_MIB = 32
WROWS = D // SAMPLES
EXTRA = 16
ROWS = CT + EXTRA
SCALE = HD ** (-0.5)
LOG2E = math.log2(math.e)
NT = (((1,), (1,)), ((), ()))
TN = (((0,), (0,)), ((), ()))


def params(mib):
    return pltpu.CompilerParams(vmem_limit_bytes=mib * 2**20)


def dot(a, b, dims=(((1,), (0,)), ((), ()))):
    return lax.dot_general(a, b, dims, preferred_element_type=F32)


def square_rows(total):
    hi = total.astype(BF16).astype(F32)
    full = jnp.concatenate([total, jnp.zeros((1, HALF - CT), F32)], axis=1)
    top = jnp.concatenate([hi, jnp.zeros((1, HALF - CT), F32)], axis=1)
    row = lax.broadcasted_iota(jnp.int32, (EXTRA, HALF), 0)
    return jnp.where(row == 0, top, jnp.where(row == 1, full - top, 0.0)).astype(BF16)


def read_squares(block):
    return jnp.sum(block[:, :CT].astype(F32), axis=0, keepdims=True)


def sort_kernel(assign_ref, x_ref, out_ref):
    for c in range(SAMPLES):
        out_ref[assign_ref[c]] = x_ref[c]


def sort_captions(assignment, x):
    vmem = pl.BlockSpec(memory_space=pltpu.VMEM)
    return pl.pallas_call(
        sort_kernel,
        in_specs=[pl.BlockSpec(memory_space=pltpu.SMEM), vmem],
        out_specs=vmem,
        out_shape=jax.ShapeDtypeStruct(x.shape, x.dtype),
        compiler_params=params(SORT_MIB),
        name="sort_captions",
    )(assignment, x)


def fetch_kernel(*refs):
    sources, targets, sems = refs[:2], refs[2:4], refs[4]
    moves = [
        pltpu.make_async_copy(source, target, sems.at[i])
        for i, (source, target) in enumerate(zip(sources, targets))
    ]
    for move in moves:
        move.start()
    for move in moves:
        move.wait()


def fetch(*arrays):
    return pl.pallas_call(
        fetch_kernel,
        in_specs=[pl.BlockSpec(memory_space=pl.ANY)] * 2,
        out_specs=[pl.BlockSpec(memory_space=pltpu.VMEM)] * 2,
        out_shape=[jax.ShapeDtypeStruct(a.shape, a.dtype) for a in arrays],
        scratch_shapes=[pltpu.SemaphoreType.DMA((2,))],
        compiler_params=params(FETCH_MIB),
        name="fetch",
    )(*arrays)


def send_kernel(core_ref, x_ref, gain_ref, w_ref, out_ref, xg_ref, sq_ref):
    @pl.when(pl.program_id(0) == 0)
    def _():
        values = x_ref[...].astype(F32)
        xg_ref[...] = (values * gain_ref[...]).astype(BF16)
        squares = jnp.sum(values * values, axis=1, keepdims=True)
        sq_ref[...] = jnp.broadcast_to(squares, (CT, 128)).T[:8, :]

    out_ref[0, :CT, :] = dot(xg_ref[...], w_ref[...]).astype(BF16)
    out_ref[0, CT:, :] = square_rows(sq_ref[:1, :])


def send_part(core, x, gain, w):
    whole = lambda i, _: (0, 0)
    return pl.pallas_call(
        send_kernel,
        grid_spec=pltpu.PrefetchScalarGridSpec(
            num_scalar_prefetch=1,
            grid=(NZH,),
            in_specs=[
                pl.BlockSpec((CT, FEAT), whole),
                pl.BlockSpec((1, FEAT), whole),
                pl.BlockSpec((FEAT, HALF), lambda i, c: (0, i * NC + 1 - c[0])),
            ],
            out_specs=[
                pl.BlockSpec((1, ROWS, HALF), lambda i, _: (i, 0, 0)),
                pl.BlockSpec((CT, FEAT), whole),
                pl.BlockSpec((8, CT), whole),
            ],
        ),
        out_shape=[
            jax.ShapeDtypeStruct((NZH, ROWS, HALF), BF16),
            jax.ShapeDtypeStruct((CT, FEAT), BF16),
            jax.ShapeDtypeStruct((8, CT), F32),
        ],
        compiler_params=params(16),
        name="text_other_half",
    )(core, x, gain, w)


def keep_kernel(core_ref, xg_ref, sq_ref, w_ref, got_ref, out_ref):
    total = dot(xg_ref[...], w_ref[...]) + got_ref[0, :CT, :].astype(F32)
    out_ref[0, :CT, :] = total.astype(BF16)
    out_ref[0, CT:, :] = square_rows(sq_ref[:1, :] + read_squares(got_ref[0, CT:, :]))


def keep_part(core, xg, sq, w, got):
    block = pl.BlockSpec((1, ROWS, HALF), lambda i, _: (i, 0, 0))
    return pl.pallas_call(
        keep_kernel,
        grid_spec=pltpu.PrefetchScalarGridSpec(
            num_scalar_prefetch=1,
            grid=(NZH,),
            in_specs=[
                pl.BlockSpec((CT, FEAT), lambda i, _: (0, 0)),
                pl.BlockSpec((8, CT), lambda i, _: (0, 0)),
                pl.BlockSpec((FEAT, HALF), lambda i, c: (0, i * NC + c[0])),
                block,
            ],
            out_specs=block,
        ),
        out_shape=jax.ShapeDtypeStruct((NZH, ROWS, HALF), BF16),
        compiler_params=params(16),
        name="text_own_half",
    )(core, xg, sq, w, got)


def text_kernel(got_ref, out_ref):
    total = got_ref[0].astype(F32)
    for i in range(1, NZH):
        total = total + got_ref[i].astype(F32)
    scale = lax.rsqrt(read_squares(total[CT:, :]) / D_ENC + 1e-06)
    column = jnp.broadcast_to(scale, (128, CT)).T[:, :1]
    out_ref[...] = (total[:CT, :] * column).astype(BF16)


def finish_text(got):
    return pl.pallas_call(
        text_kernel,
        out_shape=jax.ShapeDtypeStruct((CT, HALF), BF16),
        compiler_params=params(16),
        name="finish_text",
    )(got)


def image_kernel(q_ref, k_ref, v_ref, *refs, block, rows):
    o_ref, ml_ref, wide = refs[-3:]
    factor = SCALE * LOG2E
    wide[:, :HD] = v_ref[...]
    wide[:, HD:] = jnp.ones((IK, HD), BF16)
    lane = lax.broadcasted_iota(jnp.int32, (rows, HD), 1)
    for r in range(IQ // rows):
        part = pl.ds(r * rows, rows)
        q = q_ref[part, :]
        top = None
        for j in range(IK // block):
            cols = pl.ds(j * block, block)
            s = dot(q, k_ref[cols, :], NT)
            here = jnp.max(s, axis=1, keepdims=True) * factor
            new = here if top is None else jnp.maximum(top, here)
            p = jnp.exp2(s * factor - new).astype(BF16)
            add = dot(p, wide[cols, :])
            acc = add if top is None else acc * jnp.exp2(top - new) + add
            top = new
        o_ref[part, :] = acc[:, :HD]
        ml_ref[part, :] = jnp.where(lane < HD // 2, top, acc[:, HD:])


def image_attention(q, k, v, heads, before):
    column = lambda i: (0, heads[0] + i)
    return pl.pallas_call(
        functools.partial(image_kernel, block=512, rows=256),
        grid=(len(heads),),
        in_specs=[
            pl.BlockSpec((IQ, HD), column),
            pl.BlockSpec((IK, HD), column),
            pl.BlockSpec((IK, HD), column),
        ]
        + [pl.BlockSpec(memory_space=pl.ANY)] * len(before),
        out_specs=[pl.BlockSpec((IQ, HD), column)] * 2,
        out_shape=[jax.ShapeDtypeStruct((IQ, COLS), F32)] * 2,
        scratch_shapes=[pltpu.VMEM((IK, 2 * HD), BF16)],
        input_output_aliases={3 + i: i for i in range(len(before))},
        cost_estimate=pl.CostEstimate(flops=1, bytes_accessed=1, transcendentals=0),
        compiler_params=params(IMAGE_MIB),
        name="image_attention",
    )(q, k, v, *before)


def head_attention(length, key_pre, value_pre, q, g, gain, image_sum, stats):
    factor = SCALE * LOG2E
    keep = lax.broadcasted_iota(jnp.int32, (CT, 1), 0) < length
    turned = stats.T
    m, l = turned[:1, :], turned[HD // 2 : HD // 2 + 1, :]
    value = value_pre.astype(BF16)
    root = lax.rsqrt(jnp.mean(key_pre * key_pre, axis=1, keepdims=True) + 1e-06)
    key = (key_pre * root * gain).astype(BF16)
    s = jnp.where(keep, dot(key, q, NT) * factor, -1e30)
    top = jnp.maximum(m, jnp.max(s, axis=0, keepdims=True))
    e = jnp.exp2(s - top)
    fade = jnp.exp2(m - top)
    inverse = 1.0 / (l * fade + jnp.sum(e, axis=0, keepdims=True))
    p = e * inverse
    probs = p.astype(BF16)
    image_scale = jnp.broadcast_to(fade * inverse, (HD, IQ)).T
    joint = image_sum * image_scale + dot(probs, value, TN)
    mean = jnp.sum((g.astype(F32) * joint).T, axis=0, keepdims=True)
    ds = (p * (dot(value, g, NT) - mean) * SCALE).astype(BF16)
    d_value = dot(probs, g).astype(BF16)
    d_key = dot(ds, q).astype(BF16).astype(F32) * gain
    along = jnp.mean(d_key * key_pre, axis=1, keepdims=True)
    d_pre = (root * d_key - key_pre * (root * root * root * along)).astype(BF16)
    return joint, d_pre, d_value


def text_side_kernel(length_ref, place_ref, gain_ref, *refs):
    whole, blocks = refs[:6], refs[6 : 6 + NY + NX]
    out_ref, cot_ref = refs[6 + NY + NX : 8 + NY + NX]
    local = refs[8 + NY + NX : 14 + NY + NX]
    w, kv, joined, cots, in_sems, w_sems, out_sems, cot_sems = refs[14 + NY + NX :]
    own, other, q, g, image_sum, stats = local
    y, zl, x, core = (place_ref[i] for i in range(4))

    fetch = [
        pltpu.make_async_copy(source, target, in_sems.at[i])
        for i, (source, target) in enumerate(zip(whole, local))
    ]
    for i in range(2):
        fetch[i].start()
    order = (0, 1, 3, 2)
    moves = {s: [] for s in order}
    for s in order:
        for n in range(2):
            for r in range(NX):
                far, near = (s, r) if n == 0 else (r, s)
                for t in range(NZL):
                    half = zl if t == 0 else 1 - zl
                    target = w.at[s, half, (x + NX - r) % NX, :, n * COLS : (n + 1) * COLS]
                    source = blocks[n * 4 + far].at[near, t]
                    move = pltpu.make_async_copy(source, target, w_sems.at[s, len(moves[s])])
                    move.start()
                    moves[s].append(move)
    for i in range(2, 6):
        fetch[i].start()

    for i in range(2):
        fetch[i].wait()
    for s in order:
        for move in moves[s]:
            move.wait()
        plane = (y + NY - s) % NY
        own_w = w[s, core].reshape(HALF, 2 * COLS)
        other_w = w[s, 1 - core].reshape(HALF, 2 * COLS)
        part = dot(own[plane], own_w) + dot(other[plane], other_w)
        if s == 0:
            kv[...] = part
        else:
            kv[...] += part

    for i in range(2, 6):
        fetch[i].wait()
    leave = []
    for h in range(HEADS):
        cols = slice(h * HD, (h + 1) * HD)
        joint, d_pre, d_value = head_attention(
            length_ref[0],
            kv[:, cols],
            kv[:, COLS + h * HD : COLS + (h + 1) * HD],
            q[:, cols],
            g[:, cols],
            gain_ref[...],
            image_sum[:, cols],
            stats[:, cols],
        )
        for n, value in ((0, d_pre), (1, d_value)):
            span = slice(n * COLS + h * HD, n * COLS + (h + 1) * HD)
            cots[:, span] = value
            for i in range(NY):
                leave.append(
                    pltpu.make_async_copy(
                        cots.at[:, span], cot_ref.at[i, :, span], cot_sems.at[h, n, i]
                    )
                )
                leave[-1].start()
        joined[:, cols] = joint
        leave.append(
            pltpu.make_async_copy(joined.at[:, cols], out_ref.at[:, cols], out_sems.at[h])
        )
        leave[-1].start()
    for move in leave:
        move.wait()


def text_side(length, place, gain, own, other, q, g, image_sum, stats, keys, values):
    smem = pl.BlockSpec(memory_space=pltpu.SMEM)
    anywhere = pl.BlockSpec(memory_space=pl.ANY)
    whole = [own, other, q, g, image_sum, stats]
    return pl.pallas_call(
        text_side_kernel,
        in_specs=[smem, smem, pl.BlockSpec(memory_space=pltpu.VMEM)]
        + [anywhere] * (len(whole) + NY + NX),
        out_specs=[anywhere, anywhere],
        out_shape=[
            jax.ShapeDtypeStruct((IQ, COLS), F32),
            jax.ShapeDtypeStruct((NY, CT, 2 * COLS), BF16),
        ],
        scratch_shapes=[pltpu.VMEM(a.shape, a.dtype) for a in whole]
        + [
            pltpu.VMEM((NY, NZL, NX, WROWS, 2 * COLS), BF16),
            pltpu.VMEM((CT, 2 * COLS), F32),
            pltpu.VMEM((IQ, COLS), F32),
            pltpu.VMEM((CT, 2 * COLS), BF16),
            pltpu.SemaphoreType.DMA((len(whole),)),
            pltpu.SemaphoreType.DMA((NY, 2 * NX * NZL)),
            pltpu.SemaphoreType.DMA((HEADS,)),
            pltpu.SemaphoreType.DMA((HEADS, 2, NY)),
        ],
        compiler_params=params(56),
        name="text_side",
    )(length, place, gain, *whole, *keys, *values)


def turn_kernel(core_ref, own_ref, other_ref, out_ref):
    core = core_ref[0]
    for i, ref in ((0, own_ref), (1, other_ref)):
        half = core if i == 0 else 1 - core
        out_ref[pl.ds(pl.multiple_of(half * HALF, HALF), HALF), :] = ref[...].T


def turn(core, own, other):
    return pl.pallas_call(
        turn_kernel,
        in_specs=[pl.BlockSpec(memory_space=pltpu.SMEM)]
        + [pl.BlockSpec(memory_space=pltpu.VMEM)] * 2,
        out_shape=jax.ShapeDtypeStruct((CHUNK, NY * CT), BF16),
        compiler_params=params(16),
        name="turn_text",
    )(core, own, other)


def gradient_kernel(text_ref, cot_ref, out_ref):
    out_ref[...] = dot(text_ref[...], cot_ref[...]).astype(BF16)


def gradient(text, cot):
    steps = 2
    return pl.pallas_call(
        gradient_kernel,
        grid=(steps,),
        in_specs=[
            pl.BlockSpec((CHUNK // steps, NY * CT), lambda i: (i, 0)),
            pl.BlockSpec((NY * CT, 2 * COLS), lambda i: (0, 0)),
        ],
        out_specs=pl.BlockSpec((CHUNK // steps, 2 * COLS), lambda i: (i, 0)),
        out_shape=jax.ShapeDtypeStruct((CHUNK, 2 * COLS), BF16),
        compiler_params=params(16),
        name="gradient",
    )(text, cot)


def body(
    enc_resid,
    enc_gain,
    text_in_w,
    key_w,
    value_w,
    key_gain,
    img_query,
    img_keys,
    img_values,
    out_grad,
    cap_lengths,
    assignment,
):
    core = lax.axis_index("c").astype(jnp.int32).reshape(1)
    zl = lax.axis_index("zl")
    sample = (lax.axis_index("y") * NZL + zl) * NX + lax.axis_index("x")
    length = jnp.sum(jnp.where(assignment == sample, cap_lengths, 0)).reshape(1)
    swap = [(0, 1), (1, 0)]
    tie = lax.optimization_barrier

    place = jnp.stack([lax.axis_index(n).astype(jnp.int32) for n in ("y", "zl", "x", "c")])

    def ring(step):
        return [(i, (i + step) % 4) for i in range(4)]

    def image(heads, query, before=()):
        return tuple(image_attention(query, img_keys, img_values, heads, before))

    def around(pair, axis):
        block = jnp.stack(pair)
        two, one, three = [lax.ppermute(block, axis, ring(k)) for k in (2, 1, 3)]
        return [block, one, two, three]

    def beside(block, axis):
        return [lax.ppermute(block, axis, ring(k)) for k in (1, 3)]

    key_pair = [key_w, lax.ppermute(key_w, "zl", swap)]
    value_pair = [value_w, lax.ppermute(value_w, "zl", swap)]

    mine = sort_captions(assignment, enc_resid)
    mine = lax.all_to_all(mine, ("y", "zl", "x"), 0, 0, tiled=True)
    text_w, gain = fetch(text_in_w, enc_gain.reshape(1, FEAT))
    mine, text_w, gain, key_pair, value_pair = tie((mine, text_w, gain, key_pair, value_pair))
    send, xg, sq = send_part(core, mine.reshape(CT, FEAT), gain, text_w)
    summed = keep_part(core, xg, sq, text_w, lax.ppermute(send, "c", swap))

    summed, key_pair, value_pair = tie((summed, key_pair, value_pair))
    got = lax.all_to_all(summed, "zh", 0, 0, tiled=True)
    key_x = jnp.stack(around(key_pair, "x"))
    value_y = jnp.stack(around(value_pair, "y"))
    key_1, key_3 = beside(key_x, "y")
    value_1, value_3 = beside(value_y, "x")
    got, length, place = tie((got, length, place))

    text = finish_text(got)
    spread = jnp.broadcast_to(text.reshape(1, CT, HALF), (NZH, CT, HALF))
    spread, query = tie((spread, img_query))
    own = lax.all_to_all(spread, "zh", 0, 0, tiled=True)
    part = image((0,), query)
    part, query, key_1, key_3, value_1, value_3 = tie(
        (part, query, key_1, key_3, value_1, value_3)
    )
    key_2 = lax.ppermute(key_1, "y", ring(1))
    value_2 = lax.ppermute(value_3, "x", ring(3))
    part = image((1, 2), query, part)
    own, (o, ml), key_2, value_2 = tie((own, part, key_2, value_2))
    other = lax.ppermute(own, "c", swap)
    own_group = lax.all_to_all(own, "y", 0, 0, tiled=True).reshape(NY * CT, HALF)
    attn_out, cot = text_side(
        length,
        place,
        key_gain.reshape(1, HD),
        own,
        other,
        img_query,
        out_grad,
        o,
        ml,
        (key_x, key_1, key_2, key_3),
        (value_y, value_1, value_2, value_3),
    )
    cot, own_group = tie((cot, own_group))
    other_group = lax.ppermute(own_group, "c", swap)
    cot = lax.all_to_all(cot, "y", 0, 0, tiled=True)
    turned = turn(core, own_group, other_group)
    cot, turned = tie((cot, turned))
    cot = cot.reshape(NY * CT, 2 * COLS)
    grad = gradient(turned, cot).reshape(GROUP, WROWS, 2 * COLS)
    grad = lax.all_to_all(grad, ("zl", "x"), 0, 0, tiled=True)
    total = jnp.sum(grad.astype(F32), axis=0)
    return (attn_out, total[:, :COLS], total[:, COLS:])


def solution(mesh):
    fine = Mesh(mesh.devices.reshape(NY, NZL, NX, NZH, NC), ("y", "zl", "x", "zh", "c"))
    dp, mp = ("y", "zl", "x"), ("zh", "c")
    return jax.shard_map(
        body,
        mesh=fine,
        in_specs=(
            P(None, dp, mp),
            P(mp),
            P(mp, None),
            P(dp, mp),
            P(dp, mp),
            P(),
            P(dp, mp),
            P(dp, mp),
            P(dp, mp),
            P(dp, mp),
            P(),
            P(),
        ),
        out_specs=(P(dp, mp), P(dp, mp), P(dp, mp)),
        check_vma=False,
    )
```

```python
import functools
import math

import jax
import jax.numpy as jnp
from jax import lax
from jax.experimental import pallas as pl
from jax.experimental.pallas import tpu as pltpu
from jax.sharding import Mesh, PartitionSpec as P

BF16 = jnp.bfloat16
F32 = jnp.float32

D_ENC = 4096
D = 3072
HD = 128
CT = 256
IQ = 768
IK = 4096
SAMPLES = 32
NY, NZL, NX, NZH, NC = 4, 2, 4, 4, 2
TOK = CT // SAMPLES
FEAT = D_ENC // (NZH * NC)
COLS = D // (NZH * NC)
HEADS = COLS // HD
CHUNK = D // NY
HALF = CHUNK // NC
GROUP = NZL * NX
IMAGE_MIB = 56
SORT_MIB = 56
FETCH_MIB = 32
WROWS = D // SAMPLES
EXTRA = 16
ROWS = CT + EXTRA
SCALE = HD ** (-0.5)
LOG2E = math.log2(math.e)
NT = (((1,), (1,)), ((), ()))
TN = (((0,), (0,)), ((), ()))


def params(mib):
    return pltpu.CompilerParams(vmem_limit_bytes=mib * 2**20)


def dot(a, b, dims=(((1,), (0,)), ((), ()))):
    return lax.dot_general(a, b, dims, preferred_element_type=F32)


def square_rows(total):
    hi = total.astype(BF16).astype(F32)
    full = jnp.concatenate([total, jnp.zeros((1, HALF - CT), F32)], axis=1)
    top = jnp.concatenate([hi, jnp.zeros((1, HALF - CT), F32)], axis=1)
    row = lax.broadcasted_iota(jnp.int32, (EXTRA, HALF), 0)
    return jnp.where(row == 0, top, jnp.where(row == 1, full - top, 0.0)).astype(BF16)


def read_squares(block):
    return jnp.sum(block[:, :CT].astype(F32), axis=0, keepdims=True)


def sort_kernel(assign_ref, x_ref, out_ref):
    for c in range(SAMPLES):
        out_ref[assign_ref[c]] = x_ref[c]


def sort_captions(assignment, x):
    vmem = pl.BlockSpec(memory_space=pltpu.VMEM)
    return pl.pallas_call(
        sort_kernel,
        in_specs=[pl.BlockSpec(memory_space=pltpu.SMEM), vmem],
        out_specs=vmem,
        out_shape=jax.ShapeDtypeStruct(x.shape, x.dtype),
        compiler_params=params(SORT_MIB),
        name="sort_captions",
    )(assignment, x)


def fetch_kernel(*refs):
    sources, targets, sems = refs[:2], refs[2:4], refs[4]
    moves = [
        pltpu.make_async_copy(source, target, sems.at[i])
        for i, (source, target) in enumerate(zip(sources, targets))
    ]
    for move in moves:
        move.start()
    for move in moves:
        move.wait()


def fetch(*arrays):
    return pl.pallas_call(
        fetch_kernel,
        in_specs=[pl.BlockSpec(memory_space=pl.ANY)] * 2,
        out_specs=[pl.BlockSpec(memory_space=pltpu.VMEM)] * 2,
        out_shape=[jax.ShapeDtypeStruct(a.shape, a.dtype) for a in arrays],
        scratch_shapes=[pltpu.SemaphoreType.DMA((2,))],
        compiler_params=params(FETCH_MIB),
        name="fetch",
    )(*arrays)


def send_kernel(core_ref, x_ref, gain_ref, w_ref, out_ref, xg_ref, sq_ref):
    @pl.when(pl.program_id(0) == 0)
    def _():
        values = x_ref[...].astype(F32)
        xg_ref[...] = (values * gain_ref[...]).astype(BF16)
        squares = jnp.sum(values * values, axis=1, keepdims=True)
        sq_ref[...] = jnp.broadcast_to(squares, (CT, 128)).T[:8, :]

    out_ref[0, :CT, :] = dot(xg_ref[...], w_ref[...]).astype(BF16)
    out_ref[0, CT:, :] = square_rows(sq_ref[:1, :])


def send_part(core, x, gain, w):
    whole = lambda i, _: (0, 0)
    return pl.pallas_call(
        send_kernel,
        grid_spec=pltpu.PrefetchScalarGridSpec(
            num_scalar_prefetch=1,
            grid=(NZH,),
            in_specs=[
                pl.BlockSpec((CT, FEAT), whole),
                pl.BlockSpec((1, FEAT), whole),
                pl.BlockSpec((FEAT, HALF), lambda i, c: (0, i * NC + 1 - c[0])),
            ],
            out_specs=[
                pl.BlockSpec((1, ROWS, HALF), lambda i, _: (i, 0, 0)),
                pl.BlockSpec((CT, FEAT), whole),
                pl.BlockSpec((8, CT), whole),
            ],
        ),
        out_shape=[
            jax.ShapeDtypeStruct((NZH, ROWS, HALF), BF16),
            jax.ShapeDtypeStruct((CT, FEAT), BF16),
            jax.ShapeDtypeStruct((8, CT), F32),
        ],
        compiler_params=params(16),
        name="text_other_half",
    )(core, x, gain, w)


def keep_kernel(core_ref, xg_ref, sq_ref, w_ref, got_ref, out_ref):
    total = dot(xg_ref[...], w_ref[...]) + got_ref[0, :CT, :].astype(F32)
    out_ref[0, :CT, :] = total.astype(BF16)
    out_ref[0, CT:, :] = square_rows(sq_ref[:1, :] + read_squares(got_ref[0, CT:, :]))


def keep_part(core, xg, sq, w, got):
    block = pl.BlockSpec((1, ROWS, HALF), lambda i, _: (i, 0, 0))
    return pl.pallas_call(
        keep_kernel,
        grid_spec=pltpu.PrefetchScalarGridSpec(
            num_scalar_prefetch=1,
            grid=(NZH,),
            in_specs=[
                pl.BlockSpec((CT, FEAT), lambda i, _: (0, 0)),
                pl.BlockSpec((8, CT), lambda i, _: (0, 0)),
                pl.BlockSpec((FEAT, HALF), lambda i, c: (0, i * NC + c[0])),
                block,
            ],
            out_specs=block,
        ),
        out_shape=jax.ShapeDtypeStruct((NZH, ROWS, HALF), BF16),
        compiler_params=params(16),
        name="text_own_half",
    )(core, xg, sq, w, got)


def text_kernel(got_ref, out_ref):
    total = got_ref[0].astype(F32)
    for i in range(1, NZH):
        total = total + got_ref[i].astype(F32)
    scale = lax.rsqrt(read_squares(total[CT:, :]) / D_ENC + 1e-06)
    column = jnp.broadcast_to(scale, (128, CT)).T[:, :1]
    out_ref[...] = (total[:CT, :] * column).astype(BF16)


def finish_text(got):
    return pl.pallas_call(
        text_kernel,
        out_shape=jax.ShapeDtypeStruct((CT, HALF), BF16),
        compiler_params=params(16),
        name="finish_text",
    )(got)


def image_kernel(q_ref, k_ref, v_ref, *refs, block, rows):
    o_ref, ml_ref, wide = refs[-3:]
    factor = SCALE * LOG2E
    wide[:, :HD] = v_ref[...]
    wide[:, HD:] = jnp.ones((IK, HD), BF16)
    lane = lax.broadcasted_iota(jnp.int32, (rows, HD), 1)
    for r in range(IQ // rows):
        part = pl.ds(r * rows, rows)
        q = q_ref[part, :]
        top = None
        for j in range(IK // block):
            cols = pl.ds(j * block, block)
            s = dot(q, k_ref[cols, :], NT)
            here = jnp.max(s, axis=1, keepdims=True) * factor
            new = here if top is None else jnp.maximum(top, here)
            p = jnp.exp2(s * factor - new).astype(BF16)
            add = dot(p, wide[cols, :])
            acc = add if top is None else acc * jnp.exp2(top - new) + add
            top = new
        o_ref[part, :] = acc[:, :HD]
        ml_ref[part, :] = jnp.where(lane < HD // 2, top, acc[:, HD:])


def image_attention(q, k, v, heads, before):
    column = lambda i: (0, heads[0] + i)
    return pl.pallas_call(
        functools.partial(image_kernel, block=512, rows=256),
        grid=(len(heads),),
        in_specs=[
            pl.BlockSpec((IQ, HD), column),
            pl.BlockSpec((IK, HD), column),
            pl.BlockSpec((IK, HD), column),
        ]
        + [pl.BlockSpec(memory_space=pl.ANY)] * len(before),
        out_specs=[pl.BlockSpec((IQ, HD), column)] * 2,
        out_shape=[jax.ShapeDtypeStruct((IQ, COLS), F32)] * 2,
        scratch_shapes=[pltpu.VMEM((IK, 2 * HD), BF16)],
        input_output_aliases={3 + i: i for i in range(len(before))},
        cost_estimate=pl.CostEstimate(flops=1, bytes_accessed=1, transcendentals=0),
        compiler_params=params(IMAGE_MIB),
        name="image_attention",
    )(q, k, v, *before)


def heads_attention(length, key_pres, values, qs, gs, gain, image_sums, stats):
    factor = SCALE * LOG2E
    every = range(HEADS)
    keep = lax.broadcasted_iota(jnp.int32, (CT, 1), 0) < length
    roots = [
        lax.rsqrt(jnp.mean(k * k, axis=1, keepdims=True) + 1e-06) for k in key_pres
    ]
    keys = [(key_pres[h] * roots[h] * gain).astype(BF16) for h in every]
    scores = [jnp.where(keep, dot(keys[h], qs[h], NT) * factor, -1e30) for h in every]
    turned = [a.T for a in stats]
    tops = [
        jnp.maximum(turned[h][:1, :], jnp.max(scores[h], axis=0, keepdims=True)) for h in every
    ]
    exps = [jnp.exp2(scores[h] - tops[h]) for h in every]
    fades = [jnp.exp2(turned[h][:1, :] - tops[h]) for h in every]
    inverses = [
        1.0
        / (
            turned[h][HD // 2 : HD // 2 + 1, :] * fades[h]
            + jnp.sum(exps[h], axis=0, keepdims=True)
        )
        for h in every
    ]
    ps = [exps[h] * inverses[h] for h in every]
    probs = [p.astype(BF16) for p in ps]
    scales = [jnp.broadcast_to(fades[h] * inverses[h], (HD, IQ)).T for h in every]
    joints = [image_sums[h] * scales[h] + dot(probs[h], values[h], TN) for h in every]
    means = [
        jnp.sum((gs[h].astype(F32) * joints[h]).T, axis=0, keepdims=True) for h in every
    ]
    d_probs = [dot(values[h], gs[h], NT) for h in every]
    ds = [(ps[h] * (d_probs[h] - means[h]) * SCALE).astype(BF16) for h in every]
    d_values = [dot(probs[h], gs[h]).astype(BF16) for h in every]
    d_keys = [dot(ds[h], qs[h]).astype(BF16).astype(F32) * gain for h in every]
    d_pres = []
    for h in every:
        root, key_pre, d_key = roots[h], key_pres[h], d_keys[h]
        along = jnp.mean(d_key * key_pre, axis=1, keepdims=True)
        d_pres.append(
            (root * d_key - key_pre * (root * root * root * along)).astype(BF16)
        )
    return joints, d_pres, d_values


def text_side_kernel(length_ref, place_ref, gain_ref, *refs):
    whole, blocks = refs[:6], refs[6 : 6 + NY + NX]
    out_ref, cot_ref = refs[6 + NY + NX : 8 + NY + NX]
    local = refs[8 + NY + NX : 14 + NY + NX]
    w, kv, joined, cots, in_sems, w_sems, out_sems, cot_sems = refs[14 + NY + NX :]
    own, other, q, g, image_sum, stats = local
    y, zl, x, core = (place_ref[i] for i in range(4))

    fetch = [
        pltpu.make_async_copy(source, target, in_sems.at[i])
        for i, (source, target) in enumerate(zip(whole, local))
    ]
    for i in range(2):
        fetch[i].start()
    order = (0, 1, 3, 2)
    moves = {s: [] for s in order}
    for s in order:
        for n in range(2):
            for r in range(NX):
                far, near = (s, r) if n == 0 else (r, s)
                for t in range(NZL):
                    half = zl if t == 0 else 1 - zl
                    target = w.at[s, half, (x + NX - r) % NX, :, n * COLS : (n + 1) * COLS]
                    source = blocks[n * 4 + far].at[near, t]
                    move = pltpu.make_async_copy(source, target, w_sems.at[s, len(moves[s])])
                    move.start()
                    moves[s].append(move)
    for i in range(2, 6):
        fetch[i].start()

    for i in range(2):
        fetch[i].wait()
    for s in order:
        for move in moves[s]:
            move.wait()
        plane = (y + NY - s) % NY
        own_w = w[s, core].reshape(HALF, 2 * COLS)
        other_w = w[s, 1 - core].reshape(HALF, 2 * COLS)
        part = dot(own[plane], own_w) + dot(other[plane], other_w)
        if s == 0:
            kv[...] = part
        else:
            kv[...] += part

    for i in range(2, 6):
        fetch[i].wait()
    columns = [slice(h * HD, (h + 1) * HD) for h in range(HEADS)]
    joints, d_pres, d_values = heads_attention(
        length_ref[0],
        [kv[:, cols] for cols in columns],
        [kv[:, COLS + h * HD : COLS + (h + 1) * HD].astype(BF16) for h in range(HEADS)],
        [q[:, cols] for cols in columns],
        [g[:, cols] for cols in columns],
        gain_ref[...],
        [image_sum[:, cols] for cols in columns],
        [stats[:, cols] for cols in columns],
    )
    leave = []
    for h, cols in enumerate(columns):
        joint, d_pre, d_value = joints[h], d_pres[h], d_values[h]
        for n, value in ((0, d_pre), (1, d_value)):
            span = slice(n * COLS + h * HD, n * COLS + (h + 1) * HD)
            cots[:, span] = value
            for i in range(NY):
                leave.append(
                    pltpu.make_async_copy(
                        cots.at[:, span], cot_ref.at[i, :, span], cot_sems.at[h, n, i]
                    )
                )
                leave[-1].start()
        joined[:, cols] = joint
        leave.append(
            pltpu.make_async_copy(joined.at[:, cols], out_ref.at[:, cols], out_sems.at[h])
        )
        leave[-1].start()
    for move in leave:
        move.wait()


def text_side(length, place, gain, own, other, q, g, image_sum, stats, keys, values):
    smem = pl.BlockSpec(memory_space=pltpu.SMEM)
    anywhere = pl.BlockSpec(memory_space=pl.ANY)
    whole = [own, other, q, g, image_sum, stats]
    return pl.pallas_call(
        text_side_kernel,
        in_specs=[smem, smem, pl.BlockSpec(memory_space=pltpu.VMEM)]
        + [anywhere] * (len(whole) + NY + NX),
        out_specs=[anywhere, anywhere],
        out_shape=[
            jax.ShapeDtypeStruct((IQ, COLS), F32),
            jax.ShapeDtypeStruct((NY, CT, 2 * COLS), BF16),
        ],
        scratch_shapes=[pltpu.VMEM(a.shape, a.dtype) for a in whole]
        + [
            pltpu.VMEM((NY, NZL, NX, WROWS, 2 * COLS), BF16),
            pltpu.VMEM((CT, 2 * COLS), F32),
            pltpu.VMEM((IQ, COLS), F32),
            pltpu.VMEM((CT, 2 * COLS), BF16),
            pltpu.SemaphoreType.DMA((len(whole),)),
            pltpu.SemaphoreType.DMA((NY, 2 * NX * NZL)),
            pltpu.SemaphoreType.DMA((HEADS,)),
            pltpu.SemaphoreType.DMA((HEADS, 2, NY)),
        ],
        compiler_params=params(56),
        name="text_side",
    )(length, place, gain, *whole, *keys, *values)


def turn_kernel(core_ref, own_ref, other_ref, out_ref):
    core = core_ref[0]
    for i, ref in ((0, own_ref), (1, other_ref)):
        half = core if i == 0 else 1 - core
        out_ref[pl.ds(pl.multiple_of(half * HALF, HALF), HALF), :] = ref[...].T


def turn(core, own, other):
    return pl.pallas_call(
        turn_kernel,
        in_specs=[pl.BlockSpec(memory_space=pltpu.SMEM)]
        + [pl.BlockSpec(memory_space=pltpu.VMEM)] * 2,
        out_shape=jax.ShapeDtypeStruct((CHUNK, NY * CT), BF16),
        compiler_params=params(16),
        name="turn_text",
    )(core, own, other)


def gradient_kernel(text_ref, cot_ref, out_ref):
    out_ref[...] = dot(text_ref[...], cot_ref[...]).astype(BF16)


def gradient(text, cot):
    steps = 2
    return pl.pallas_call(
        gradient_kernel,
        grid=(steps,),
        in_specs=[
            pl.BlockSpec((CHUNK // steps, NY * CT), lambda i: (i, 0)),
            pl.BlockSpec((NY * CT, 2 * COLS), lambda i: (0, 0)),
        ],
        out_specs=pl.BlockSpec((CHUNK // steps, 2 * COLS), lambda i: (i, 0)),
        out_shape=jax.ShapeDtypeStruct((CHUNK, 2 * COLS), BF16),
        compiler_params=params(16),
        name="gradient",
    )(text, cot)


def body(
    enc_resid,
    enc_gain,
    text_in_w,
    key_w,
    value_w,
    key_gain,
    img_query,
    img_keys,
    img_values,
    out_grad,
    cap_lengths,
    assignment,
):
    core = lax.axis_index("c").astype(jnp.int32).reshape(1)
    zl = lax.axis_index("zl")
    sample = (lax.axis_index("y") * NZL + zl) * NX + lax.axis_index("x")
    length = jnp.sum(jnp.where(assignment == sample, cap_lengths, 0)).reshape(1)
    swap = [(0, 1), (1, 0)]
    tie = lax.optimization_barrier

    place = jnp.stack([lax.axis_index(n).astype(jnp.int32) for n in ("y", "zl", "x", "c")])

    def ring(step):
        return [(i, (i + step) % 4) for i in range(4)]

    def image(heads, query, before=()):
        return tuple(image_attention(query, img_keys, img_values, heads, before))

    def around(pair, axis):
        block = jnp.stack(pair)
        two, one, three = [lax.ppermute(block, axis, ring(k)) for k in (2, 1, 3)]
        return [block, one, two, three]

    def beside(block, axis):
        return [lax.ppermute(block, axis, ring(k)) for k in (1, 3)]

    key_pair = [key_w, lax.ppermute(key_w, "zl", swap)]
    value_pair = [value_w, lax.ppermute(value_w, "zl", swap)]

    mine = sort_captions(assignment, enc_resid)
    mine = lax.all_to_all(mine, ("y", "zl", "x"), 0, 0, tiled=True)
    text_w, gain = fetch(text_in_w, enc_gain.reshape(1, FEAT))
    mine, text_w, gain, key_pair, value_pair = tie((mine, text_w, gain, key_pair, value_pair))
    send, xg, sq = send_part(core, mine.reshape(CT, FEAT), gain, text_w)
    summed = keep_part(core, xg, sq, text_w, lax.ppermute(send, "c", swap))

    summed, key_pair, value_pair = tie((summed, key_pair, value_pair))
    got = lax.all_to_all(summed, "zh", 0, 0, tiled=True)
    key_x = jnp.stack(around(key_pair, "x"))
    value_y = jnp.stack(around(value_pair, "y"))
    key_1, key_3 = beside(key_x, "y")
    value_1, value_3 = beside(value_y, "x")
    got, length, place = tie((got, length, place))

    text = finish_text(got)
    spread = jnp.broadcast_to(text.reshape(1, CT, HALF), (NZH, CT, HALF))
    spread, query = tie((spread, img_query))
    own = lax.all_to_all(spread, "zh", 0, 0, tiled=True)
    part = image((0,), query)
    part, query, key_1, key_3, value_1, value_3 = tie(
        (part, query, key_1, key_3, value_1, value_3)
    )
    key_2 = lax.ppermute(key_1, "y", ring(1))
    value_2 = lax.ppermute(value_3, "x", ring(3))
    part = image((1, 2), query, part)
    own, (o, ml), key_2, value_2 = tie((own, part, key_2, value_2))
    other = lax.ppermute(own, "c", swap)
    own_group = lax.all_to_all(own, "y", 0, 0, tiled=True).reshape(NY * CT, HALF)
    attn_out, cot = text_side(
        length,
        place,
        key_gain.reshape(1, HD),
        own,
        other,
        img_query,
        out_grad,
        o,
        ml,
        (key_x, key_1, key_2, key_3),
        (value_y, value_1, value_2, value_3),
    )
    cot, own_group = tie((cot, own_group))
    other_group = lax.ppermute(own_group, "c", swap)
    cot = lax.all_to_all(cot, "y", 0, 0, tiled=True)
    turned = turn(core, own_group, other_group)
    cot, turned = tie((cot, turned))
    cot = cot.reshape(NY * CT, 2 * COLS)
    grad = gradient(turned, cot).reshape(GROUP, WROWS, 2 * COLS)
    grad = lax.all_to_all(grad, ("zl", "x"), 0, 0, tiled=True)
    total = jnp.sum(grad.astype(F32), axis=0)
    return (attn_out, total[:, :COLS], total[:, COLS:])


def solution(mesh):
    fine = Mesh(mesh.devices.reshape(NY, NZL, NX, NZH, NC), ("y", "zl", "x", "zh", "c"))
    dp, mp = ("y", "zl", "x"), ("zh", "c")
    return jax.shard_map(
        body,
        mesh=fine,
        in_specs=(
            P(None, dp, mp),
            P(mp),
            P(mp, None),
            P(dp, mp),
            P(dp, mp),
            P(),
            P(dp, mp),
            P(dp, mp),
            P(dp, mp),
            P(dp, mp),
            P(),
            P(),
        ),
        out_specs=(P(dp, mp), P(dp, mp), P(dp, mp)),
        check_vma=False,
    )
```

```python
import functools
import math

import jax
import jax.numpy as jnp
from jax import lax
from jax.experimental import pallas as pl
from jax.experimental.pallas import tpu as pltpu
from jax.sharding import Mesh, PartitionSpec as P

BF16 = jnp.bfloat16
F32 = jnp.float32

D_ENC = 4096
D = 3072
HD = 128
CT = 256
IQ = 768
IK = 4096
SAMPLES = 32
NY, NZL, NX, NZH, NC = 4, 2, 4, 4, 2
TOK = CT // SAMPLES
FEAT = D_ENC // (NZH * NC)
COLS = D // (NZH * NC)
HEADS = COLS // HD
CHUNK = D // NY
HALF = CHUNK // NC
GROUP = NZL * NX
IMAGE_MIB = 56
SORT_MIB = 56
FETCH_MIB = 32
WROWS = D // SAMPLES
EXTRA = 16
ROWS = CT + EXTRA
SCALE = HD ** (-0.5)
LOG2E = math.log2(math.e)
NT = (((1,), (1,)), ((), ()))
TN = (((0,), (0,)), ((), ()))


def params(mib):
    return pltpu.CompilerParams(vmem_limit_bytes=mib * 2**20)


def dot(a, b, dims=(((1,), (0,)), ((), ()))):
    return lax.dot_general(a, b, dims, preferred_element_type=F32)


def square_rows(total):
    hi = total.astype(BF16).astype(F32)
    full = jnp.concatenate([total, jnp.zeros((1, HALF - CT), F32)], axis=1)
    top = jnp.concatenate([hi, jnp.zeros((1, HALF - CT), F32)], axis=1)
    row = lax.broadcasted_iota(jnp.int32, (EXTRA, HALF), 0)
    return jnp.where(row == 0, top, jnp.where(row == 1, full - top, 0.0)).astype(BF16)


def read_squares(block):
    return jnp.sum(block[:, :CT].astype(F32), axis=0, keepdims=True)


def sort_kernel(assign_ref, x_ref, out_ref):
    for c in range(SAMPLES):
        out_ref[assign_ref[c]] = x_ref[c]


def sort_captions(assignment, x):
    vmem = pl.BlockSpec(memory_space=pltpu.VMEM)
    return pl.pallas_call(
        sort_kernel,
        in_specs=[pl.BlockSpec(memory_space=pltpu.SMEM), vmem],
        out_specs=vmem,
        out_shape=jax.ShapeDtypeStruct(x.shape, x.dtype),
        compiler_params=params(SORT_MIB),
        name="sort_captions",
    )(assignment, x)


def fetch_kernel(*refs):
    sources, targets, sems = refs[:2], refs[2:4], refs[4]
    moves = [
        pltpu.make_async_copy(source, target, sems.at[i])
        for i, (source, target) in enumerate(zip(sources, targets))
    ]
    for move in moves:
        move.start()
    for move in moves:
        move.wait()


def fetch(*arrays):
    return pl.pallas_call(
        fetch_kernel,
        in_specs=[pl.BlockSpec(memory_space=pl.ANY)] * 2,
        out_specs=[pl.BlockSpec(memory_space=pltpu.VMEM)] * 2,
        out_shape=[jax.ShapeDtypeStruct(a.shape, a.dtype) for a in arrays],
        scratch_shapes=[pltpu.SemaphoreType.DMA((2,))],
        compiler_params=params(FETCH_MIB),
        name="fetch",
    )(*arrays)


def send_kernel(core_ref, x_ref, gain_ref, w_ref, out_ref, xg_ref, sq_ref):
    @pl.when(pl.program_id(0) == 0)
    def _():
        values = x_ref[...].astype(F32)
        xg_ref[...] = (values * gain_ref[...]).astype(BF16)
        squares = jnp.sum(values * values, axis=1, keepdims=True)
        sq_ref[...] = jnp.broadcast_to(squares, (CT, 128)).T[:8, :]

    out_ref[0, :CT, :] = dot(xg_ref[...], w_ref[...]).astype(BF16)
    out_ref[0, CT:, :] = square_rows(sq_ref[:1, :])


def send_part(core, x, gain, w):
    whole = lambda i, _: (0, 0)
    return pl.pallas_call(
        send_kernel,
        grid_spec=pltpu.PrefetchScalarGridSpec(
            num_scalar_prefetch=1,
            grid=(NZH,),
            in_specs=[
                pl.BlockSpec((CT, FEAT), whole),
                pl.BlockSpec((1, FEAT), whole),
                pl.BlockSpec((FEAT, HALF), lambda i, c: (0, i * NC + 1 - c[0])),
            ],
            out_specs=[
                pl.BlockSpec((1, ROWS, HALF), lambda i, _: (i, 0, 0)),
                pl.BlockSpec((CT, FEAT), whole),
                pl.BlockSpec((8, CT), whole),
            ],
        ),
        out_shape=[
            jax.ShapeDtypeStruct((NZH, ROWS, HALF), BF16),
            jax.ShapeDtypeStruct((CT, FEAT), BF16),
            jax.ShapeDtypeStruct((8, CT), F32),
        ],
        compiler_params=params(16),
        name="text_other_half",
    )(core, x, gain, w)


def keep_kernel(core_ref, xg_ref, sq_ref, w_ref, got_ref, out_ref):
    total = dot(xg_ref[...], w_ref[...]) + got_ref[0, :CT, :].astype(F32)
    out_ref[0, :CT, :] = total.astype(BF16)
    out_ref[0, CT:, :] = square_rows(sq_ref[:1, :] + read_squares(got_ref[0, CT:, :]))


def keep_part(core, xg, sq, w, got):
    block = pl.BlockSpec((1, ROWS, HALF), lambda i, _: (i, 0, 0))
    return pl.pallas_call(
        keep_kernel,
        grid_spec=pltpu.PrefetchScalarGridSpec(
            num_scalar_prefetch=1,
            grid=(NZH,),
            in_specs=[
                pl.BlockSpec((CT, FEAT), lambda i, _: (0, 0)),
                pl.BlockSpec((8, CT), lambda i, _: (0, 0)),
                pl.BlockSpec((FEAT, HALF), lambda i, c: (0, i * NC + c[0])),
                block,
            ],
            out_specs=block,
        ),
        out_shape=jax.ShapeDtypeStruct((NZH, ROWS, HALF), BF16),
        compiler_params=params(16),
        name="text_own_half",
    )(core, xg, sq, w, got)


def text_kernel(got_ref, out_ref):
    total = got_ref[0].astype(F32)
    for i in range(1, NZH):
        total = total + got_ref[i].astype(F32)
    scale = lax.rsqrt(read_squares(total[CT:, :]) / D_ENC + 1e-06)
    column = jnp.broadcast_to(scale, (128, CT)).T[:, :1]
    out_ref[...] = (total[:CT, :] * column).astype(BF16)


def finish_text(got):
    return pl.pallas_call(
        text_kernel,
        out_shape=jax.ShapeDtypeStruct((CT, HALF), BF16),
        compiler_params=params(16),
        name="finish_text",
    )(got)


def image_kernel(q_ref, k_ref, v_ref, *refs, block, rows):
    o_ref, ml_ref, wide = refs[-3:]
    factor = SCALE * LOG2E
    wide[:, :HD] = v_ref[...]
    wide[:, HD:] = jnp.ones((IK, HD), BF16)
    lane = lax.broadcasted_iota(jnp.int32, (rows, HD), 1)
    for r in range(IQ // rows):
        part = pl.ds(r * rows, rows)
        q = q_ref[part, :]
        top = None
        for j in range(IK // block):
            cols = pl.ds(j * block, block)
            s = dot(q, k_ref[cols, :], NT)
            here = jnp.max(s, axis=1, keepdims=True) * factor
            new = here if top is None else jnp.maximum(top, here)
            p = jnp.exp2(s * factor - new).astype(BF16)
            add = dot(p, wide[cols, :])
            acc = add if top is None else acc * jnp.exp2(top - new) + add
            top = new
        o_ref[part, :] = acc[:, :HD]
        ml_ref[part, :] = jnp.where(lane < HD // 2, top, acc[:, HD:])


def image_attention(q, k, v, heads, before):
    column = lambda i: (0, heads[0] + i)
    return pl.pallas_call(
        functools.partial(image_kernel, block=256, rows=384),
        grid=(len(heads),),
        in_specs=[
            pl.BlockSpec((IQ, HD), column),
            pl.BlockSpec((IK, HD), column),
            pl.BlockSpec((IK, HD), column),
        ]
        + [pl.BlockSpec(memory_space=pl.ANY)] * len(before),
        out_specs=[pl.BlockSpec((IQ, HD), column)] * 2,
        out_shape=[jax.ShapeDtypeStruct((IQ, COLS), F32)] * 2,
        scratch_shapes=[pltpu.VMEM((IK, 2 * HD), BF16)],
        input_output_aliases={3 + i: i for i in range(len(before))},
        cost_estimate=pl.CostEstimate(flops=1, bytes_accessed=1, transcendentals=0),
        compiler_params=params(IMAGE_MIB),
        name="image_attention",
    )(q, k, v, *before)


def heads_attention(
    length, key_pres, values, qs, gs, gain, image_sums, stats, leave_joint, leave_cot
):
    factor = SCALE * LOG2E
    every = range(HEADS)
    keep = lax.broadcasted_iota(jnp.int32, (CT, 1), 0) < length
    roots = [
        lax.rsqrt(jnp.mean(k * k, axis=1, keepdims=True) + 1e-06) for k in key_pres
    ]
    keys = [(key_pres[h] * roots[h] * gain).astype(BF16) for h in every]
    scores = [jnp.where(keep, dot(keys[h], qs[h], NT) * factor, -1e30) for h in every]
    turned = [a.T for a in stats]
    tops = [
        jnp.maximum(turned[h][:1, :], jnp.max(scores[h], axis=0, keepdims=True)) for h in every
    ]
    exps = [jnp.exp2(scores[h] - tops[h]) for h in every]
    fades = [jnp.exp2(turned[h][:1, :] - tops[h]) for h in every]
    inverses = [
        1.0
        / (
            turned[h][HD // 2 : HD // 2 + 1, :] * fades[h]
            + jnp.sum(exps[h], axis=0, keepdims=True)
        )
        for h in every
    ]
    ps = [exps[h] * inverses[h] for h in every]
    probs = [p.astype(BF16) for p in ps]
    scales = [jnp.broadcast_to(fades[h] * inverses[h], (HD, IQ)).T for h in every]
    joints = [image_sums[h] * scales[h] + dot(probs[h], values[h], TN) for h in every]
    for h in every:
        leave_joint(h, joints[h])
    d_values = [dot(probs[h], gs[h]).astype(BF16) for h in every]
    for h in every:
        leave_cot(h, 1, d_values[h])
    means = [
        jnp.sum((gs[h].astype(F32) * joints[h]).T, axis=0, keepdims=True) for h in every
    ]
    d_probs = [dot(values[h], gs[h], NT) for h in every]
    ds = [(ps[h] * (d_probs[h] - means[h]) * SCALE).astype(BF16) for h in every]
    d_keys = [dot(ds[h], qs[h]).astype(BF16).astype(F32) * gain for h in every]
    for h in every:
        root, key_pre, d_key = roots[h], key_pres[h], d_keys[h]
        along = jnp.mean(d_key * key_pre, axis=1, keepdims=True)
        d_pre = root * d_key - key_pre * (root * root * root * along)
        leave_cot(h, 0, d_pre.astype(BF16))


def text_side_kernel(length_ref, place_ref, gain_ref, *refs):
    whole, blocks = refs[:6], refs[6 : 6 + NY + NX]
    out_ref, cot_ref = refs[6 + NY + NX : 8 + NY + NX]
    local = refs[8 + NY + NX : 14 + NY + NX]
    w, kv, joined, cots, in_sems, w_sems, out_sems, cot_sems = refs[14 + NY + NX :]
    own, other, q, g, image_sum, stats = local
    y, zl, x, core = (place_ref[i] for i in range(4))

    fetch = [
        pltpu.make_async_copy(source, target, in_sems.at[i])
        for i, (source, target) in enumerate(zip(whole, local))
    ]
    for i in range(2):
        fetch[i].start()
    order = (0, 1, 3, 2)
    moves = {s: [] for s in order}
    for s in order:
        for n in range(2):
            for r in range(NX):
                far, near = (s, r) if n == 0 else (r, s)
                for t in range(NZL):
                    half = zl if t == 0 else 1 - zl
                    target = w.at[s, half, (x + NX - r) % NX, :, n * COLS : (n + 1) * COLS]
                    source = blocks[n * 4 + far].at[near, t]
                    move = pltpu.make_async_copy(source, target, w_sems.at[s, len(moves[s])])
                    move.start()
                    moves[s].append(move)
    for i in range(2, 6):
        fetch[i].start()

    for i in range(2):
        fetch[i].wait()
    for s in order:
        for move in moves[s]:
            move.wait()
        plane = (y + NY - s) % NY
        own_w = w[s, core].reshape(HALF, 2 * COLS)
        other_w = w[s, 1 - core].reshape(HALF, 2 * COLS)
        part = dot(own[plane], own_w) + dot(other[plane], other_w)
        if s == 0:
            kv[...] = part
        else:
            kv[...] += part

    for i in range(2, 6):
        fetch[i].wait()
    columns = [slice(h * HD, (h + 1) * HD) for h in range(HEADS)]
    leave = []

    def leave_joint(h, joint):
        joined[:, columns[h]] = joint
        leave.append(
            pltpu.make_async_copy(
                joined.at[:, columns[h]], out_ref.at[:, columns[h]], out_sems.at[h]
            )
        )
        leave[-1].start()

    def leave_cot(h, n, value):
        span = slice(n * COLS + h * HD, n * COLS + (h + 1) * HD)
        cots[:, span] = value
        for i in range(NY):
            leave.append(
                pltpu.make_async_copy(
                    cots.at[:, span], cot_ref.at[i, :, span], cot_sems.at[h, n, i]
                )
            )
            leave[-1].start()

    heads_attention(
        length_ref[0],
        [kv[:, cols] for cols in columns],
        [kv[:, COLS + h * HD : COLS + (h + 1) * HD].astype(BF16) for h in range(HEADS)],
        [q[:, cols] for cols in columns],
        [g[:, cols] for cols in columns],
        gain_ref[...],
        [image_sum[:, cols] for cols in columns],
        [stats[:, cols] for cols in columns],
        leave_joint,
        leave_cot,
    )
    for move in leave:
        move.wait()


def text_side(length, place, gain, own, other, q, g, image_sum, stats, keys, values):
    smem = pl.BlockSpec(memory_space=pltpu.SMEM)
    anywhere = pl.BlockSpec(memory_space=pl.ANY)
    whole = [own, other, q, g, image_sum, stats]
    return pl.pallas_call(
        text_side_kernel,
        in_specs=[smem, smem, pl.BlockSpec(memory_space=pltpu.VMEM)]
        + [anywhere] * (len(whole) + NY + NX),
        out_specs=[anywhere, anywhere],
        out_shape=[
            jax.ShapeDtypeStruct((IQ, COLS), F32),
            jax.ShapeDtypeStruct((NY, CT, 2 * COLS), BF16),
        ],
        scratch_shapes=[pltpu.VMEM(a.shape, a.dtype) for a in whole]
        + [
            pltpu.VMEM((NY, NZL, NX, WROWS, 2 * COLS), BF16),
            pltpu.VMEM((CT, 2 * COLS), F32),
            pltpu.VMEM((IQ, COLS), F32),
            pltpu.VMEM((CT, 2 * COLS), BF16),
            pltpu.SemaphoreType.DMA((len(whole),)),
            pltpu.SemaphoreType.DMA((NY, 2 * NX * NZL)),
            pltpu.SemaphoreType.DMA((HEADS,)),
            pltpu.SemaphoreType.DMA((HEADS, 2, NY)),
        ],
        compiler_params=params(56),
        name="text_side",
    )(length, place, gain, *whole, *keys, *values)


def turn_kernel(core_ref, own_ref, other_ref, out_ref):
    core = core_ref[0]
    for i, ref in ((0, own_ref), (1, other_ref)):
        half = core if i == 0 else 1 - core
        out_ref[pl.ds(pl.multiple_of(half * HALF, HALF), HALF), :] = ref[...].T


def turn(core, own, other):
    return pl.pallas_call(
        turn_kernel,
        in_specs=[pl.BlockSpec(memory_space=pltpu.SMEM)]
        + [pl.BlockSpec(memory_space=pltpu.VMEM)] * 2,
        out_shape=jax.ShapeDtypeStruct((CHUNK, NY * CT), BF16),
        compiler_params=params(16),
        name="turn_text",
    )(core, own, other)


def gradient_kernel(text_ref, cot_ref, out_ref):
    out_ref[...] = dot(text_ref[...], cot_ref[...]).astype(BF16)


def gradient(text, cot):
    steps = 2
    return pl.pallas_call(
        gradient_kernel,
        grid=(steps,),
        in_specs=[
            pl.BlockSpec((CHUNK // steps, NY * CT), lambda i: (i, 0)),
            pl.BlockSpec((NY * CT, 2 * COLS), lambda i: (0, 0)),
        ],
        out_specs=pl.BlockSpec((CHUNK // steps, 2 * COLS), lambda i: (i, 0)),
        out_shape=jax.ShapeDtypeStruct((CHUNK, 2 * COLS), BF16),
        compiler_params=params(16),
        name="gradient",
    )(text, cot)


def body(
    enc_resid,
    enc_gain,
    text_in_w,
    key_w,
    value_w,
    key_gain,
    img_query,
    img_keys,
    img_values,
    out_grad,
    cap_lengths,
    assignment,
):
    core = lax.axis_index("c").astype(jnp.int32).reshape(1)
    zl = lax.axis_index("zl")
    sample = (lax.axis_index("y") * NZL + zl) * NX + lax.axis_index("x")
    length = jnp.sum(jnp.where(assignment == sample, cap_lengths, 0)).reshape(1)
    swap = [(0, 1), (1, 0)]
    tie = lax.optimization_barrier

    place = jnp.stack([lax.axis_index(n).astype(jnp.int32) for n in ("y", "zl", "x", "c")])

    def ring(step):
        return [(i, (i + step) % 4) for i in range(4)]

    def image(heads, query, before=()):
        return tuple(image_attention(query, img_keys, img_values, heads, before))

    def around(pair, axis):
        block = jnp.stack(pair)
        two, one, three = [lax.ppermute(block, axis, ring(k)) for k in (2, 1, 3)]
        return [block, one, two, three]

    def beside(block, axis):
        return [lax.ppermute(block, axis, ring(k)) for k in (1, 3)]

    key_pair = [key_w, lax.ppermute(key_w, "zl", swap)]
    value_pair = [value_w, lax.ppermute(value_w, "zl", swap)]

    mine = sort_captions(assignment, enc_resid)
    mine = lax.all_to_all(mine, ("y", "zl", "x"), 0, 0, tiled=True)
    text_w, gain = fetch(text_in_w, enc_gain.reshape(1, FEAT))
    mine, text_w, gain, key_pair, value_pair = tie((mine, text_w, gain, key_pair, value_pair))
    send, xg, sq = send_part(core, mine.reshape(CT, FEAT), gain, text_w)
    summed = keep_part(core, xg, sq, text_w, lax.ppermute(send, "c", swap))

    summed, key_pair, value_pair = tie((summed, key_pair, value_pair))
    got = lax.all_to_all(summed, "zh", 0, 0, tiled=True)
    key_x = jnp.stack(around(key_pair, "x"))
    value_y = jnp.stack(around(value_pair, "y"))
    key_1, key_3 = beside(key_x, "y")
    value_1, value_3 = beside(value_y, "x")
    got, length, place = tie((got, length, place))

    text = finish_text(got)
    spread = jnp.broadcast_to(text.reshape(1, CT, HALF), (NZH, CT, HALF))
    spread, query = tie((spread, img_query))
    own = lax.all_to_all(spread, "zh", 0, 0, tiled=True)
    part = image((0,), query)
    part, query, key_1, key_3, value_1, value_3 = tie(
        (part, query, key_1, key_3, value_1, value_3)
    )
    key_2 = lax.ppermute(key_1, "y", ring(1))
    value_2 = lax.ppermute(value_3, "x", ring(3))
    part = image((1, 2), query, part)
    own, (o, ml), key_2, value_2 = tie((own, part, key_2, value_2))
    other = lax.ppermute(own, "c", swap)
    own_group = lax.all_to_all(own, "y", 0, 0, tiled=True).reshape(NY * CT, HALF)
    attn_out, cot = text_side(
        length,
        place,
        key_gain.reshape(1, HD),
        own,
        other,
        img_query,
        out_grad,
        o,
        ml,
        (key_x, key_1, key_2, key_3),
        (value_y, value_1, value_2, value_3),
    )
    cot, own_group = tie((cot, own_group))
    other_group = lax.ppermute(own_group, "c", swap)
    cot = lax.all_to_all(cot, "y", 0, 0, tiled=True)
    turned = turn(core, own_group, other_group)
    cot, turned = tie((cot, turned))
    cot = cot.reshape(NY * CT, 2 * COLS)
    grad = gradient(turned, cot).reshape(GROUP, WROWS, 2 * COLS)
    grad = lax.all_to_all(grad, ("zl", "x"), 0, 0, tiled=True)
    total = jnp.sum(grad.astype(F32), axis=0)
    return (attn_out, total[:, :COLS], total[:, COLS:])


def solution(mesh):
    fine = Mesh(mesh.devices.reshape(NY, NZL, NX, NZH, NC), ("y", "zl", "x", "zh", "c"))
    dp, mp = ("y", "zl", "x"), ("zh", "c")
    return jax.shard_map(
        body,
        mesh=fine,
        in_specs=(
            P(None, dp, mp),
            P(mp),
            P(mp, None),
            P(dp, mp),
            P(dp, mp),
            P(),
            P(dp, mp),
            P(dp, mp),
            P(dp, mp),
            P(dp, mp),
            P(),
            P(),
        ),
        out_specs=(P(dp, mp), P(dp, mp), P(dp, mp)),
        check_vma=False,
    )
```

```python
import functools
import math

import jax
import jax.numpy as jnp
from jax import lax
from jax.experimental import pallas as pl
from jax.experimental.pallas import tpu as pltpu
from jax.sharding import Mesh, PartitionSpec as P

BF16 = jnp.bfloat16
F32 = jnp.float32

D_ENC = 4096
D = 3072
HD = 128
CT = 256
IQ = 768
IK = 4096
SAMPLES = 32
NY, NZL, NX, NZH, NC = 4, 2, 4, 4, 2
TOK = CT // SAMPLES
FEAT = D_ENC // (NZH * NC)
COLS = D // (NZH * NC)
HEADS = COLS // HD
CHUNK = D // NY
HALF = CHUNK // NC
GROUP = NZL * NX
IMAGE_MIB = 56
SORT_MIB = 56
FETCH_MIB = 32
WROWS = D // SAMPLES
EXTRA = 16
ROWS = CT + EXTRA
SCALE = HD ** (-0.5)
LOG2E = math.log2(math.e)
NT = (((1,), (1,)), ((), ()))
TN = (((0,), (0,)), ((), ()))


def params(mib):
    return pltpu.CompilerParams(vmem_limit_bytes=mib * 2**20)


def dot(a, b, dims=(((1,), (0,)), ((), ()))):
    return lax.dot_general(a, b, dims, preferred_element_type=F32)


def square_rows(total):
    hi = total.astype(BF16).astype(F32)
    full = jnp.concatenate([total, jnp.zeros((1, HALF - CT), F32)], axis=1)
    top = jnp.concatenate([hi, jnp.zeros((1, HALF - CT), F32)], axis=1)
    row = lax.broadcasted_iota(jnp.int32, (EXTRA, HALF), 0)
    return jnp.where(row == 0, top, jnp.where(row == 1, full - top, 0.0)).astype(BF16)


def read_squares(block):
    return jnp.sum(block[:, :CT].astype(F32), axis=0, keepdims=True)


def sort_kernel(assign_ref, x_ref, out_ref):
    for c in range(SAMPLES):
        out_ref[assign_ref[c]] = x_ref[c]


def sort_captions(assignment, x):
    vmem = pl.BlockSpec(memory_space=pltpu.VMEM)
    return pl.pallas_call(
        sort_kernel,
        in_specs=[pl.BlockSpec(memory_space=pltpu.SMEM), vmem],
        out_specs=vmem,
        out_shape=jax.ShapeDtypeStruct(x.shape, x.dtype),
        compiler_params=params(SORT_MIB),
        name="sort_captions",
    )(assignment, x)


def fetch_kernel(*refs):
    sources, targets, sems = refs[:2], refs[2:4], refs[4]
    moves = [
        pltpu.make_async_copy(source, target, sems.at[i])
        for i, (source, target) in enumerate(zip(sources, targets))
    ]
    for move in moves:
        move.start()
    for move in moves:
        move.wait()


def fetch(*arrays):
    return pl.pallas_call(
        fetch_kernel,
        in_specs=[pl.BlockSpec(memory_space=pl.ANY)] * 2,
        out_specs=[pl.BlockSpec(memory_space=pltpu.VMEM)] * 2,
        out_shape=[jax.ShapeDtypeStruct(a.shape, a.dtype) for a in arrays],
        scratch_shapes=[pltpu.SemaphoreType.DMA((2,))],
        compiler_params=params(FETCH_MIB),
        name="fetch",
    )(*arrays)


def send_kernel(core_ref, x_ref, gain_ref, w_ref, out_ref, xg_ref, sq_ref):
    @pl.when(pl.program_id(0) == 0)
    def _():
        values = x_ref[...].astype(F32)
        xg_ref[...] = (values * gain_ref[...]).astype(BF16)
        squares = jnp.sum(values * values, axis=1, keepdims=True)
        sq_ref[...] = jnp.broadcast_to(squares, (CT, 128)).T[:8, :]

    out_ref[0, :CT, :] = dot(xg_ref[...], w_ref[...]).astype(BF16)
    out_ref[0, CT:, :] = square_rows(sq_ref[:1, :])


def send_part(core, x, gain, w):
    whole = lambda i, _: (0, 0)
    return pl.pallas_call(
        send_kernel,
        grid_spec=pltpu.PrefetchScalarGridSpec(
            num_scalar_prefetch=1,
            grid=(NZH,),
            in_specs=[
                pl.BlockSpec((CT, FEAT), whole),
                pl.BlockSpec((1, FEAT), whole),
                pl.BlockSpec((FEAT, HALF), lambda i, c: (0, i * NC + 1 - c[0])),
            ],
            out_specs=[
                pl.BlockSpec((1, ROWS, HALF), lambda i, _: (i, 0, 0)),
                pl.BlockSpec((CT, FEAT), whole),
                pl.BlockSpec((8, CT), whole),
            ],
        ),
        out_shape=[
            jax.ShapeDtypeStruct((NZH, ROWS, HALF), BF16),
            jax.ShapeDtypeStruct((CT, FEAT), BF16),
            jax.ShapeDtypeStruct((8, CT), F32),
        ],
        compiler_params=params(16),
        name="text_other_half",
    )(core, x, gain, w)


def keep_kernel(core_ref, xg_ref, sq_ref, w_ref, got_ref, out_ref):
    total = dot(xg_ref[...], w_ref[...]) + got_ref[0, :CT, :].astype(F32)
    out_ref[0, :CT, :] = total.astype(BF16)
    out_ref[0, CT:, :] = square_rows(sq_ref[:1, :] + read_squares(got_ref[0, CT:, :]))


def keep_part(core, xg, sq, w, got):
    block = pl.BlockSpec((1, ROWS, HALF), lambda i, _: (i, 0, 0))
    return pl.pallas_call(
        keep_kernel,
        grid_spec=pltpu.PrefetchScalarGridSpec(
            num_scalar_prefetch=1,
            grid=(NZH,),
            in_specs=[
                pl.BlockSpec((CT, FEAT), lambda i, _: (0, 0)),
                pl.BlockSpec((8, CT), lambda i, _: (0, 0)),
                pl.BlockSpec((FEAT, HALF), lambda i, c: (0, i * NC + c[0])),
                block,
            ],
            out_specs=block,
        ),
        out_shape=jax.ShapeDtypeStruct((NZH, ROWS, HALF), BF16),
        compiler_params=params(16),
        name="text_own_half",
    )(core, xg, sq, w, got)


def text_kernel(got_ref, out_ref):
    total = got_ref[0].astype(F32)
    for i in range(1, NZH):
        total = total + got_ref[i].astype(F32)
    scale = lax.rsqrt(read_squares(total[CT:, :]) / D_ENC + 1e-06)
    column = jnp.broadcast_to(scale, (128, CT)).T[:, :1]
    out_ref[...] = (total[:CT, :] * column).astype(BF16)


def finish_text(got):
    return pl.pallas_call(
        text_kernel,
        out_shape=jax.ShapeDtypeStruct((CT, HALF), BF16),
        compiler_params=params(16),
        name="finish_text",
    )(got)


def image_kernel(q_ref, k_ref, v_ref, *refs, block, rows):
    o_ref, ml_ref, wide = refs[-3:]
    factor = SCALE * LOG2E
    wide[:, :HD] = v_ref[...]
    wide[:, HD:] = jnp.ones((IK, HD), BF16)
    lane = lax.broadcasted_iota(jnp.int32, (rows, HD), 1)
    for r in range(IQ // rows):
        part = pl.ds(r * rows, rows)
        q = q_ref[part, :]
        top = None
        for j in range(IK // block):
            cols = pl.ds(j * block, block)
            s = dot(q, k_ref[cols, :], NT)
            here = jnp.max(s, axis=1, keepdims=True) * factor
            new = here if top is None else jnp.maximum(top, here)
            p = jnp.exp2(s * factor - new).astype(BF16)
            add = dot(p, wide[cols, :])
            acc = add if top is None else acc * jnp.exp2(top - new) + add
            top = new
        o_ref[part, :] = acc[:, :HD]
        ml_ref[part, :] = jnp.where(lane < HD // 2, top, acc[:, HD:])


def image_attention(q, k, v, heads, before):
    column = lambda i: (0, heads[0] + i)
    return pl.pallas_call(
        functools.partial(image_kernel, block=256, rows=384),
        grid=(len(heads),),
        in_specs=[
            pl.BlockSpec((IQ, HD), column),
            pl.BlockSpec((IK, HD), column),
            pl.BlockSpec((IK, HD), column),
        ]
        + [pl.BlockSpec(memory_space=pl.ANY)] * len(before),
        out_specs=[pl.BlockSpec((IQ, HD), column)] * 2,
        out_shape=[jax.ShapeDtypeStruct((IQ, COLS), F32)] * 2,
        scratch_shapes=[pltpu.VMEM((IK, 2 * HD), BF16)],
        input_output_aliases={3 + i: i for i in range(len(before))},
        cost_estimate=pl.CostEstimate(flops=1, bytes_accessed=1, transcendentals=0),
        compiler_params=params(IMAGE_MIB),
        name="image_attention",
    )(q, k, v, *before)


def heads_attention(
    length, key_pres, values, qs, gs, gain, image_sums, stats, leave_joint, leave_cot
):
    factor = SCALE * LOG2E
    every = range(HEADS)
    keep = lax.broadcasted_iota(jnp.int32, (CT, 1), 0) < length
    roots = [
        lax.rsqrt(jnp.mean(k * k, axis=1, keepdims=True) + 1e-06) for k in key_pres
    ]
    keys = [(key_pres[h] * roots[h] * gain).astype(BF16) for h in every]
    scores = [jnp.where(keep, dot(keys[h], qs[h], NT) * factor, -1e30) for h in every]
    turned = [a.T for a in stats]
    tops = [
        jnp.maximum(turned[h][:1, :], jnp.max(scores[h], axis=0, keepdims=True)) for h in every
    ]
    exps = [jnp.exp2(scores[h] - tops[h]) for h in every]
    fades = [jnp.exp2(turned[h][:1, :] - tops[h]) for h in every]
    inverses = [
        1.0
        / (
            turned[h][HD // 2 : HD // 2 + 1, :] * fades[h]
            + jnp.sum(exps[h], axis=0, keepdims=True)
        )
        for h in every
    ]
    ps = [exps[h] * inverses[h] for h in every]
    probs = [p.astype(BF16) for p in ps]
    scales = [jnp.broadcast_to(fades[h] * inverses[h], (HD, IQ)).T for h in every]
    joints = [image_sums[h] * scales[h] + dot(probs[h], values[h], TN) for h in every]
    for h in every:
        leave_joint(h, joints[h])
    d_values = [dot(probs[h], gs[h]).astype(BF16) for h in every]
    for h in every:
        leave_cot(h, 1, d_values[h])
    means = [
        jnp.sum((gs[h].astype(F32) * joints[h]).T, axis=0, keepdims=True) for h in every
    ]
    d_probs = [dot(values[h], gs[h], NT) for h in every]
    ds = [(ps[h] * (d_probs[h] - means[h]) * SCALE).astype(BF16) for h in every]
    d_keys = [dot(ds[h], qs[h]).astype(BF16).astype(F32) * gain for h in every]
    for h in every:
        root, key_pre, d_key = roots[h], key_pres[h], d_keys[h]
        along = jnp.mean(d_key * key_pre, axis=1, keepdims=True)
        d_pre = root * d_key - key_pre * (root * root * root * along)
        leave_cot(h, 0, d_pre.astype(BF16))


def text_side_kernel(length_ref, place_ref, gain_ref, *refs):
    whole, blocks = refs[:6], refs[6 : 6 + NY + NX]
    out_ref, cot_ref = refs[6 + NY + NX : 8 + NY + NX]
    local = refs[8 + NY + NX : 14 + NY + NX]
    w, kv, joined, cots, in_sems, w_sems, out_sems, cot_sems = refs[14 + NY + NX :]
    own, other, q, g, image_sum, stats = local
    y, zl, x, core = (place_ref[i] for i in range(4))

    fetch = [
        pltpu.make_async_copy(source, target, in_sems.at[i])
        for i, (source, target) in enumerate(zip(whole, local))
    ]
    for i in range(2):
        fetch[i].start()
    order = (0, 1, 3, 2)
    moves = {s: [] for s in order}
    for s in order:
        for n in range(2):
            for r in range(NX):
                far, near = (s, r) if n == 0 else (r, s)
                for t in range(NZL):
                    half = zl if t == 0 else 1 - zl
                    target = w.at[s, half, (x + NX - r) % NX, :, n * COLS : (n + 1) * COLS]
                    source = blocks[n * 4 + far].at[near, t]
                    move = pltpu.make_async_copy(source, target, w_sems.at[s, len(moves[s])])
                    move.start()
                    moves[s].append(move)
    for i in range(2, 6):
        fetch[i].start()

    for i in range(2):
        fetch[i].wait()
    for s in order:
        for move in moves[s]:
            move.wait()
        plane = (y + NY - s) % NY
        own_w = w[s, core].reshape(HALF, 2 * COLS)
        other_w = w[s, 1 - core].reshape(HALF, 2 * COLS)
        part = dot(own[plane], own_w) + dot(other[plane], other_w)
        if s == 0:
            kv[...] = part
        else:
            kv[...] += part

    for i in range(2, 6):
        fetch[i].wait()
    columns = [slice(h * HD, (h + 1) * HD) for h in range(HEADS)]
    leave = []

    def leave_joint(h, joint):
        joined[:, columns[h]] = joint
        leave.append(
            pltpu.make_async_copy(
                joined.at[:, columns[h]], out_ref.at[:, columns[h]], out_sems.at[h]
            )
        )
        leave[-1].start()

    def leave_cot(h, n, value):
        span = slice(n * COLS + h * HD, n * COLS + (h + 1) * HD)
        cots[:, span] = value
        for i in range(NY):
            leave.append(
                pltpu.make_async_copy(
                    cots.at[:, span], cot_ref.at[i, :, span], cot_sems.at[h, n, i]
                )
            )
            leave[-1].start()

    heads_attention(
        length_ref[0],
        [kv[:, cols] for cols in columns],
        [kv[:, COLS + h * HD : COLS + (h + 1) * HD].astype(BF16) for h in range(HEADS)],
        [q[:, cols] for cols in columns],
        [g[:, cols] for cols in columns],
        gain_ref[...],
        [image_sum[:, cols] for cols in columns],
        [stats[:, cols] for cols in columns],
        leave_joint,
        leave_cot,
    )
    for move in leave:
        move.wait()


def text_side(length, place, gain, own, other, q, g, image_sum, stats, keys, values):
    smem = pl.BlockSpec(memory_space=pltpu.SMEM)
    anywhere = pl.BlockSpec(memory_space=pl.ANY)
    whole = [own, other, q, g, image_sum, stats]
    return pl.pallas_call(
        text_side_kernel,
        in_specs=[smem, smem, pl.BlockSpec(memory_space=pltpu.VMEM)]
        + [anywhere] * (len(whole) + NY + NX),
        out_specs=[anywhere, anywhere],
        out_shape=[
            jax.ShapeDtypeStruct((IQ, COLS), F32),
            jax.ShapeDtypeStruct((NY, CT, 2 * COLS), BF16),
        ],
        scratch_shapes=[pltpu.VMEM(a.shape, a.dtype) for a in whole]
        + [
            pltpu.VMEM((NY, NZL, NX, WROWS, 2 * COLS), BF16),
            pltpu.VMEM((CT, 2 * COLS), F32),
            pltpu.VMEM((IQ, COLS), F32),
            pltpu.VMEM((CT, 2 * COLS), BF16),
            pltpu.SemaphoreType.DMA((len(whole),)),
            pltpu.SemaphoreType.DMA((NY, 2 * NX * NZL)),
            pltpu.SemaphoreType.DMA((HEADS,)),
            pltpu.SemaphoreType.DMA((HEADS, 2, NY)),
        ],
        compiler_params=params(56),
        name="text_side",
    )(length, place, gain, *whole, *keys, *values)


def turn_kernel(core_ref, own_ref, other_ref, out_ref):
    core = core_ref[0]
    for i, ref in ((0, own_ref), (1, other_ref)):
        half = core if i == 0 else 1 - core
        out_ref[pl.ds(pl.multiple_of(half * HALF, HALF), HALF), :] = ref[...].T


def turn(core, own, other):
    return pl.pallas_call(
        turn_kernel,
        in_specs=[pl.BlockSpec(memory_space=pltpu.SMEM)]
        + [pl.BlockSpec(memory_space=pltpu.VMEM)] * 2,
        out_shape=jax.ShapeDtypeStruct((CHUNK, NY * CT), BF16),
        compiler_params=params(16),
        name="turn_text",
    )(core, own, other)


def gradient_kernel(text_ref, cot_ref, out_ref):
    out_ref[...] = dot(text_ref[...], cot_ref[...]).astype(BF16)


def gradient(text, cot):
    steps = 2
    return pl.pallas_call(
        gradient_kernel,
        grid=(steps,),
        in_specs=[
            pl.BlockSpec((CHUNK // steps, NY * CT), lambda i: (i, 0)),
            pl.BlockSpec((NY * CT, 2 * COLS), lambda i: (0, 0)),
        ],
        out_specs=pl.BlockSpec((CHUNK // steps, 2 * COLS), lambda i: (i, 0)),
        out_shape=jax.ShapeDtypeStruct((CHUNK, 2 * COLS), BF16),
        compiler_params=params(16),
        name="gradient",
    )(text, cot)


def body(
    enc_resid,
    enc_gain,
    text_in_w,
    key_w,
    value_w,
    key_gain,
    img_query,
    img_keys,
    img_values,
    out_grad,
    cap_lengths,
    assignment,
):
    core = lax.axis_index("c").astype(jnp.int32).reshape(1)
    zl = lax.axis_index("zl")
    sample = (lax.axis_index("y") * NZL + zl) * NX + lax.axis_index("x")
    length = jnp.sum(jnp.where(assignment == sample, cap_lengths, 0)).reshape(1)
    swap = [(0, 1), (1, 0)]
    tie = lax.optimization_barrier

    place = jnp.stack([lax.axis_index(n).astype(jnp.int32) for n in ("y", "zl", "x", "c")])

    def ring(step):
        return [(i, (i + step) % 4) for i in range(4)]

    def image(heads, query, before=()):
        return tuple(image_attention(query, img_keys, img_values, heads, before))

    def around(pair, axis):
        block = jnp.stack(pair)
        two, one, three = [lax.ppermute(block, axis, ring(k)) for k in (2, 1, 3)]
        return [block, one, two, three]

    def beside(block, axis):
        return [lax.ppermute(block, axis, ring(k)) for k in (1, 3)]

    key_pair = [key_w, lax.ppermute(key_w, "zl", swap)]
    value_pair = [value_w, lax.ppermute(value_w, "zl", swap)]

    mine = sort_captions(assignment, enc_resid)
    mine = lax.all_to_all(mine, ("y", "zl", "x"), 0, 0, tiled=True)
    text_w, gain = fetch(text_in_w, enc_gain.reshape(1, FEAT))
    mine, text_w, gain, key_pair = tie((mine, text_w, gain, key_pair))
    send, xg, sq = send_part(core, mine.reshape(CT, FEAT), gain, text_w)
    summed = keep_part(core, xg, sq, text_w, lax.ppermute(send, "c", swap))

    summed, key_pair, value_pair = tie((summed, key_pair, value_pair))
    got = lax.all_to_all(summed, "zh", 0, 0, tiled=True)
    key_x = jnp.stack(around(key_pair, "x"))
    value_y = jnp.stack(around(value_pair, "y"))
    key_1, key_3 = beside(key_x, "y")
    value_1, value_3 = beside(value_y, "x")
    got, length, place = tie((got, length, place))

    text = finish_text(got)
    spread = jnp.broadcast_to(text.reshape(1, CT, HALF), (NZH, CT, HALF))
    spread, query = tie((spread, img_query))
    own = lax.all_to_all(spread, "zh", 0, 0, tiled=True)
    part = image((0,), query)
    part, query, key_1, key_3, value_1, value_3 = tie(
        (part, query, key_1, key_3, value_1, value_3)
    )
    key_2 = lax.ppermute(key_1, "y", ring(1))
    value_2 = lax.ppermute(value_3, "x", ring(3))
    part = image((1, 2), query, part)
    own, (o, ml), key_2, value_2 = tie((own, part, key_2, value_2))
    other = lax.ppermute(own, "c", swap)
    own_group = lax.all_to_all(own, "y", 0, 0, tiled=True).reshape(NY * CT, HALF)
    attn_out, cot = text_side(
        length,
        place,
        key_gain.reshape(1, HD),
        own,
        other,
        img_query,
        out_grad,
        o,
        ml,
        (key_x, key_1, key_2, key_3),
        (value_y, value_1, value_2, value_3),
    )
    cot, own_group = tie((cot, own_group))
    other_group = lax.ppermute(own_group, "c", swap)
    cot = lax.all_to_all(cot, "y", 0, 0, tiled=True)
    turned = turn(core, own_group, other_group)
    cot, turned = tie((cot, turned))
    cot = cot.reshape(NY * CT, 2 * COLS)
    grad = gradient(turned, cot).reshape(GROUP, WROWS, 2 * COLS)
    grad = lax.all_to_all(grad, ("zl", "x"), 0, 0, tiled=True)
    total = jnp.sum(grad.astype(F32), axis=0)
    return (attn_out, total[:, :COLS], total[:, COLS:])


def solution(mesh):
    fine = Mesh(mesh.devices.reshape(NY, NZL, NX, NZH, NC), ("y", "zl", "x", "zh", "c"))
    dp, mp = ("y", "zl", "x"), ("zh", "c")
    return jax.shard_map(
        body,
        mesh=fine,
        in_specs=(
            P(None, dp, mp),
            P(mp),
            P(mp, None),
            P(dp, mp),
            P(dp, mp),
            P(),
            P(dp, mp),
            P(dp, mp),
            P(dp, mp),
            P(dp, mp),
            P(),
            P(),
        ),
        out_specs=(P(dp, mp), P(dp, mp), P(dp, mp)),
        check_vma=False,
    )
```
